128 devices in a mesh: group: 2 (over z_lo), seq: 16 (over x, z_hi, core), dp: 4 (over y).
Axes of the slice: x: 4, y: 4, z: 4 (z_hi: 2, z_lo: 2; z = z_hi * 2 + z_lo), core: 2. Of those that a mesh axis runs over, the one named last changes fastest.
Arguments:
- latent_tokens: bfloat16 [8, 4096, 3072], P(('group', 'dp'), 'seq'), may hold values from -6 to 6
- modulation: float32 [8, 2, 3072], P(('group', 'dp')), may hold values from -3 to 3, as said below
- w_qkv: bfloat16 [3, 3072, 2048], P(None, None, 'seq'), may hold values from -0.108253175 to 0.108253175, as said below
- w_out: bfloat16 [2048, 64], replicated, may hold values from -0.125 to 0.125
- noisy_latents: bfloat16 [8, 16, 4, 32, 128], P(('group', 'dp'), None, None, 'seq'), may hold values from -6 to 6
- queue: int32 [8], replicated, may hold values from 0 to 7, each once
- frame_counts: int32 [8], replicated, may hold values from 1 to 4, 24 in all
- conv_w: bfloat16 [512, 432], replicated, may hold values from -0.3125 to 0.3125
- conv_b: float32 [512], replicated, may hold values from -1 to 1
Outputs:
- attended: bfloat16 [8, 4096, 2048], P(('group', 'dp'), 'seq')
- decoded: bfloat16 [8, 512, 4, 32, 128], P(('group', 'dp'), None, None, 'seq')
The draws below stay inside these ranges and needn't reach their ends.
Inputs may be any that keep to these rules, and one draw needn't show every extreme that they name: `queue`: each request appears once. `frame_counts`: some request has all 4 frames. `modulation`: row 0 holds the shift, row 1 the scale. `w_qkv`: query, key and value blocks in that order.
All inputs are finite; a program needn't handle non-finite values.
Results may differ from the reference program's by a relative error of at most 0.012.
Values may be sent and summed in bfloat16 or wider, within the bound.
No kernel may reach another device: no remote copies, remote signals or barrier semaphores. Data moves between devices by JAX's collectives and lax.ppermute only.
A program may use at most 192 MiB of HBM per device.

```python
import math
import jax
import jax.numpy as jnp
import numpy as np
from jax import lax

D = 3072
HEADS = 16
HEAD_DIM = 128
LAT_C = 16
C_OUT = 512
FRAMES = 4
PCOLS = 64
REQS = 8
TOKENS = 4096
HEIGHT = 32
WIDTH = 128


def draw_modulation(key, part):
    key = jax.random.fold_in(key, 11)
    shift_key, scale_key = jax.random.split(key, 2)
    shift = 0.5 * jax.random.truncated_normal(shift_key, -6.0, 6.0, (REQS, 1, D), jnp.float32)
    scale = 0.5 * jax.random.truncated_normal(scale_key, -6.0, 6.0, (REQS, 1, D), jnp.float32)
    return jnp.concatenate([shift, scale], axis=1)


def draw_w_qkv(key, part):
    key = jax.random.fold_in(key, 12)
    base_key = jax.random.fold_in(key, 0)
    columns = HEADS * HEAD_DIM
    spread = jnp.float32(D) ** (-0.5)
    whole = jax.random.truncated_normal(base_key, -5.9, 5.9, (3, D, columns), jnp.float32) * spread
    return whole.astype(jnp.bfloat16)


def shard_levels(key, dims, pieces, low, high):
    def one(dim, parts):
        heights = jax.random.uniform(jax.random.fold_in(jax.random.fold_in(key, 6), dim), (parts,), jnp.float32, low / len(pieces), high / len(pieces))
        return jnp.repeat(jnp.exp(heights), dims[dim] // parts).reshape((-1,) + (1,) * (len(dims) - dim - 1))

    gain = one(*pieces[0])
    for cut in pieces[1:]:
        gain = gain * one(*cut)
    return gain


def length_profile(number_of, total, reach, lean):
    loads = [(1 << 20) // math.isqrt(rank ** lean) + 1 for rank in range(2, number_of + 1)]
    surplus, holding = total - reach - (number_of - 1), [1] * (number_of - 1)
    while surplus > 0:
        candidates = [i for i in range(number_of - 1) if holding[i] < reach]
        pool, budget = sum([loads[i] for i in candidates]), surplus
        for i in candidates:
            addition = min(reach - holding[i], max(1, budget * loads[i] // pool), surplus)
            holding[i] = holding[i] + addition
            surplus = surplus - addition
    return np.array([reach] + holding)


def uneven_parts(key, amount, total, most, slope):
    if amount == 2:
        one = jax.random.randint(key, (), max(1, total - most), min(most, total - 1) + 1)
        return jnp.stack([one, total - one])
    tallies = jnp.asarray(length_profile(amount, total, most, slope), jnp.int32)
    twos = (amount - 1) // 2
    source_of, taker = tallies[1:1 + 2 * twos:2], tallies[2:2 + 2 * twos:2]
    margin = jnp.minimum(source_of - 1, most - taker)
    passed = jax.random.randint(jax.random.fold_in(key, 1), (twos,), 0, 1 << 20) % (margin + 1)
    tallies = tallies.at[1:1 + 2 * twos:2].set(source_of - passed).at[2:2 + 2 * twos:2].set(taker + passed)
    return tallies[jax.random.permutation(jax.random.fold_in(key, 2), amount)]


def bell_draw(own_key, shape, deviation, bound, shards=(), kind=jnp.bfloat16):
    array = jax.random.normal(own_key, shape, jnp.float32) * deviation
    if len(shards) > 0:
        array = shard_levels(own_key, shape, shards, -0.22, 0.18) * array
    return jnp.clip(array, min=-bound, max=bound).astype(kind)


def setup_inputs(seed: int = 0) -> dict:
    seeds = jax.random.split(jax.random.key(seed), 10)
    return {
        "latent_tokens": bell_draw(seeds[0], (REQS, TOKENS, D), 1.0, 6.0, ((0, 8), (1, 16))),
        "modulation": draw_modulation(jax.random.fold_in(seeds[9], 71), 0),
        "w_qkv": draw_w_qkv(jax.random.fold_in(seeds[9], 71), 0),
        "w_out": bell_draw(seeds[3], (HEADS * HEAD_DIM, 4 * LAT_C), (HEADS * HEAD_DIM) ** -0.5, 0.125),
        "noisy_latents": bell_draw(seeds[4], (REQS, LAT_C, FRAMES, HEIGHT, WIDTH), 1.0, 6.0, ((0, 8), (3, 16))),
        "queue": jax.random.permutation(seeds[5], REQS).astype(jnp.int32),
        "frame_counts": uneven_parts(seeds[6], REQS, REQS * FRAMES * 3 // 4, FRAMES, 1).astype(jnp.int32),
        "conv_w": bell_draw(seeds[7], (C_OUT, 27 * LAT_C), (27 * LAT_C) ** -0.5, 0.3125),
        "conv_b": jnp.clip(jax.random.uniform(seeds[8], (C_OUT,), jnp.float32, -1.0, 1.0), -1.0, 1.0),
    }


def attend_request(tokens, modulation, w_qkv):
    values = tokens.astype(jnp.float32)
    scaled = values * lax.rsqrt(lax.optimization_barrier(jnp.mean(values * values, axis=-1, keepdims=True)) + 1e-06)
    normed = (scaled * (1.0 + modulation[1]) + modulation[0]).astype(jnp.bfloat16)
    qkv = jnp.einsum('td,cdh->cth', normed.astype(jnp.float32), w_qkv.astype(jnp.float32)).astype(jnp.bfloat16)
    heads = qkv.reshape(3, TOKENS, HEADS, HEAD_DIM).transpose(0, 2, 1, 3)

    def one_head(triple):
        query, keys, vals = triple
        scores = jnp.dot(query, keys.T, preferred_element_type=jnp.float32) / jnp.sqrt(jnp.float32(HEAD_DIM))
        probs = jax.nn.softmax(scores, axis=-1).astype(jnp.bfloat16)
        return jnp.dot(probs, vals, preferred_element_type=jnp.float32).astype(jnp.bfloat16)
    outputs = lax.map(one_head, (heads[0], heads[1], heads[2]))
    return outputs.transpose(1, 0, 2).reshape(TOKENS, HEADS * HEAD_DIM)

def update_latent(attended, noisy, w_out):
    values = attended.astype(jnp.float32)
    final_normed = (values * lax.rsqrt(lax.optimization_barrier(jnp.mean(values * values, axis=-1, keepdims=True)) + 1e-06)).astype(jnp.bfloat16)
    predicted = jnp.dot(final_normed, w_out, preferred_element_type=jnp.float32)
    grid = predicted.reshape(HEIGHT // 2, FRAMES, PCOLS, LAT_C, 2, 2)
    grid = grid.transpose(3, 1, 0, 4, 2, 5).reshape(LAT_C, FRAMES, HEIGHT, WIDTH)
    return (noisy.astype(jnp.float32) + grid).astype(jnp.bfloat16)

def decode_request(latent, limit, conv_w, conv_b):
    first = latent[:, :1]
    padded = jnp.concatenate([first, first, latent], axis=1)
    padded = jnp.pad(padded, ((0, 0), (0, 0), (1, 1), (1, 1)))
    slices = []
    for step_t in range(3):
        for step_h in range(3):
            for step_w in range(3):
                slices.append(padded[:, step_t:step_t + FRAMES, step_h:step_h + HEIGHT, step_w:step_w + WIDTH])
    stacked = jnp.stack(slices, 0).reshape(27 * LAT_C, FRAMES * HEIGHT * WIDTH)
    features = jnp.dot(conv_w, stacked, preferred_element_type=jnp.float32) + conv_b[:, None]
    features = features.reshape(C_OUT, FRAMES, HEIGHT, WIDTH)
    frame_ids = jnp.arange(FRAMES, dtype=jnp.int32)
    keep = (frame_ids < limit).astype(jnp.float32)
    return (features * keep[None, :, None, None]).astype(jnp.bfloat16)

def reference(latent_tokens, modulation, w_qkv, w_out, noisy_latents, queue, frame_counts, conv_w, conv_b):
    attended = lax.map(lambda pair: attend_request(pair[0], pair[1], w_qkv), (latent_tokens, modulation))
    new_latent = lax.map(lambda pair: update_latent(pair[0], pair[1], w_out), (attended, noisy_latents))

    def one_slot(source):
        latent = lax.dynamic_index_in_dim(new_latent, source, 0, keepdims=False)
        limit = lax.dynamic_index_in_dim(frame_counts, source, 0, keepdims=False)
        return decode_request(latent, limit, conv_w, conv_b)
    decoded = lax.map(one_slot, queue.astype(jnp.int32))
    return (attended, decoded)
```

```python
import functools
import math

import jax
import jax.numpy as jnp
from jax import lax
from jax.experimental import pallas as pl
from jax.experimental.pallas import tpu as pltpu
from jax.sharding import PartitionSpec as P

HEAD_DIM = 128
EVERY = ("group", "seq", "dp")
XS, ZS, YS = (4, 4, 4)
VMEM_BYTES = 48 << 20
QUERY_SCALE = math.log2(math.e) / math.sqrt(HEAD_DIM)
NT = (((1,), (1,)), ((), ()))


def linear(x, y, z, core):
    return ((z % 2) * 16 + (x * 2 + z // 2) * 2 + core) * YS + y


def moved(array, move):
    perm = []
    for x in range(XS):
        for y in range(YS):
            for z in range(ZS):
                for core in range(2):
                    to = move(x, y, z, core)
                    there = linear(to[0] % XS, to[1] % YS, to[2] % ZS, to[3])
                    perm.append((linear(x, y, z, core), there))
    return lax.ppermute(array, EVERY, perm)


def right(x, y, z, core):
    return (x + 1, y, z, core)


def left(x, y, z, core):
    return (x - 1, y, z, core)


def other_core(x, y, z, core):
    return (x, y, z, 1 - core)


def opposite_z(x, y, z, core):
    return (x, y, z + 2, core)


def mirrored_z(x, y, z, core):
    return (x, y, 3 - z, core)


def project_kernel(n_tokens, part_ref, *refs):
    tokens = refs[:n_tokens]
    w_ref = refs[n_tokens]
    w_parts = refs[n_tokens + 1 : n_tokens + 5]
    own_ref, away_ref = refs[n_tokens + 5 :]
    total = None
    for k in range(4):
        depth = w_parts[k].shape[1]
        at = pl.multiple_of(part_ref[k] * depth, depth)
        rows = jnp.concatenate([t[:, pl.ds(at, depth)] for t in tokens], axis=0)
        columns = jnp.concatenate([w_ref[0, pl.ds(at, depth), :], w_parts[k][0]], axis=1)
        term = jnp.dot(rows, columns, preferred_element_type=jnp.float32)
        total = term if total is None else total + term
    scale = jnp.where(pl.program_id(0) == 0, jnp.float32(QUERY_SCALE), jnp.float32(1.0))
    total = (total * scale).astype(jnp.bfloat16)
    own_ref[0] = total[:, :HEAD_DIM]
    away_ref[0] = total[:, HEAD_DIM:]


def project(parts, tokens, w_qkv, w_parts):
    rows = sum(t.shape[0] for t in tokens)
    depth = w_qkv.shape[1]
    whole = pl.BlockSpec(memory_space=pltpu.VMEM)
    out = jax.ShapeDtypeStruct((3, rows, HEAD_DIM), jnp.bfloat16)
    return pl.pallas_call(
        functools.partial(project_kernel, len(tokens)),
        grid_spec=pltpu.PrefetchScalarGridSpec(
            num_scalar_prefetch=1,
            grid=(3,),
            in_specs=[whole] * len(tokens)
            + [pl.BlockSpec((1, depth, HEAD_DIM), lambda c, s: (c, 0, 0))]
            + [pl.BlockSpec((1, depth // 4, HEAD_DIM), lambda c, s: (c, 0, 0))] * 4,
            out_specs=[pl.BlockSpec((1, rows, HEAD_DIM), lambda c, s: (c, 0, 0))] * 2,
        ),
        out_shape=(out, out),
        compiler_params=pltpu.CompilerParams(vmem_limit_bytes=VMEM_BYTES),
        cost_estimate=pl.CostEstimate(
            flops=rows * depth * 6 * HEAD_DIM * 2,
            bytes_accessed=rows * depth * 2 + depth * 6 * HEAD_DIM * 2,
            transcendentals=0,
        ),
    )(parts, *tokens, w_qkv, *w_parts)


def attention_kernel(n_blocks, chunk, place_ref, *refs):
    blocks = refs[:n_blocks]
    out_ref, q_all, k_all, v_all = refs[n_blocks:]

    @pl.when(pl.program_id(0) == 0)
    def _():
        rows = blocks[0].shape[1]
        half = rows // 2
        for i, block in enumerate(blocks):
            k_all[i * rows : (i + 1) * rows, :] = block[1]
            v_all[i * rows : (i + 1) * rows, :] = block[2]
            for j in range(2):
                at = pl.multiple_of(place_ref[2 * i + j] * half, half)
                q_all[pl.ds(at, half), :] = block[0, j * half : (j + 1) * half, :]

    rows = out_ref.shape[0]
    q = q_all[pl.ds(pl.multiple_of(pl.program_id(0) * rows, rows), rows), :]
    ones = jnp.ones((chunk, HEAD_DIM), jnp.bfloat16)
    top, total = (None, None)
    for at in range(0, k_all.shape[0], chunk):
        keys = k_all[at : at + chunk, :]
        vals = jnp.concatenate([v_all[at : at + chunk, :], ones], axis=1)
        scores = lax.dot_general(q, keys, NT, preferred_element_type=jnp.float32)
        high = jnp.max(scores, axis=1, keepdims=True)
        if top is not None:
            high = jnp.maximum(top, high)
        probs = jnp.exp2(scores - high).astype(jnp.bfloat16)
        term = jnp.dot(probs, vals, preferred_element_type=jnp.float32)
        total = term if top is None else total * jnp.exp2(top - high) + term
        top = high
    out_ref[...] = (total[:, :HEAD_DIM] / total[:, HEAD_DIM:]).astype(jnp.bfloat16)


def attention(place, blocks, rows=1024, chunk=256):
    tokens = sum(b.shape[1] for b in blocks)
    whole = pl.BlockSpec(memory_space=pltpu.VMEM)
    return pl.pallas_call(
        functools.partial(attention_kernel, len(blocks), chunk),
        grid_spec=pltpu.PrefetchScalarGridSpec(
            num_scalar_prefetch=1,
            grid=(tokens // rows,),
            in_specs=[whole] * len(blocks),
            out_specs=pl.BlockSpec((rows, HEAD_DIM), lambda i, s: (i, 0)),
            scratch_shapes=[pltpu.VMEM((tokens, HEAD_DIM), jnp.bfloat16)] * 3,
        ),
        out_shape=jax.ShapeDtypeStruct((tokens, HEAD_DIM), jnp.bfloat16),
        compiler_params=pltpu.CompilerParams(vmem_limit_bytes=VMEM_BYTES),
        cost_estimate=pl.CostEstimate(
            flops=tokens * tokens * HEAD_DIM * 4,
            bytes_accessed=tokens * HEAD_DIM * 8,
            transcendentals=tokens * tokens,
        ),
    )(place, *blocks)


def padded_2(array, sides, width):
    for axis, dim in sides:
        size, length = (lax.axis_size(axis), array.shape[dim])
        up = [(i, (i + 1) % size) for i in range(size - 1)]
        down = [(j, i) for i, j in up]
        last = lax.slice_in_dim(array, length - width, length, axis=dim)
        initial = lax.slice_in_dim(array, 0, width, axis=dim)
        before = lax.ppermute(last, axis, up)
        after = lax.ppermute(initial, axis, down)
        array = jnp.concatenate([before, array, after], axis=dim)
    return array


def update_rows(attended, noisy, w_out):
    values = attended.astype(jnp.float32)
    final_normed = (
        values * lax.rsqrt(jnp.mean(values * values, axis=-1, keepdims=True) + 1e-06)
    ).astype(jnp.bfloat16)
    predicted = jnp.dot(final_normed, w_out, preferred_element_type=jnp.float32)
    channels = noisy.shape[0]
    frames = noisy.shape[1]
    rows = noisy.shape[2]
    columns = noisy.shape[3]
    grid = predicted.reshape(rows // 2, frames, columns // 2, channels, 2, 2)
    grid = grid.transpose(3, 1, 0, 4, 2, 5).reshape(channels, frames, rows, columns)
    return (noisy.astype(jnp.float32) + grid).astype(jnp.bfloat16)


def causal_features(padded, limit, conv_w, conv_b):
    frames = padded.shape[1]
    rows = padded.shape[2] - 2
    columns = padded.shape[3]
    first = padded[:, :1]
    padded = jnp.concatenate([first, first, padded], axis=1)
    padded = jnp.pad(padded, ((0, 0), (0, 0), (0, 0), (1, 1)))
    slices = []
    for step_t in range(3):
        for step_h in range(3):
            for step_w in range(3):
                slices.append(
                    padded[
                        :,
                        step_t : step_t + frames,
                        step_h : step_h + rows,
                        step_w : step_w + columns,
                    ]
                )
    stacked = jnp.stack(slices, 0).reshape(27 * padded.shape[0], frames * rows * columns)
    features = jnp.dot(conv_w, stacked, preferred_element_type=jnp.float32) + conv_b[:, None]
    features = features.reshape(conv_w.shape[0], frames, rows, columns)
    frame_ids = jnp.arange(frames, dtype=jnp.int32)
    keep = (frame_ids < limit).astype(jnp.float32)
    return (features * keep[None, :, None, None]).astype(jnp.bfloat16)


def on_device(
    latent_tokens, modulation, w_qkv, w_out, noisy_latents, queue, frame_counts, conv_w, conv_b
):
    z_low = lax.axis_index("group")
    seat = lax.axis_index("seq")
    y = lax.axis_index("dp")
    x, z_high, core = (seat // 4, seat // 2 % 2, seat % 2)

    quarter = w_qkv.shape[1] // 4
    part = lax.dynamic_slice_in_dim(w_qkv, y * quarter, quarter, axis=1)
    part_0 = moved(part, mirrored_z)
    part_1 = moved(part_0, lambda x, y, z, core: (x, y - 1, z, core))
    part_3 = moved(part_0, lambda x, y, z, core: (x, y + 1, z, core))
    part_2 = moved(part_0, lambda x, y, z, core: (x, y + 2, z, core))
    w_parts = (part_0, part_1, part_2, part_3)
    parts = (y + jnp.arange(4, dtype=jnp.int32)) % 4

    values = latent_tokens[0].astype(jnp.float32)
    shift_scale = modulation[0]
    scaled = values * lax.rsqrt(jnp.mean(values * values, axis=-1, keepdims=True) + 1e-06)
    normed = (scaled * (1.0 + shift_scale[1]) + shift_scale[0]).astype(jnp.bfloat16)

    half = normed.shape[0] // 2
    from_left = moved(normed, right)
    from_right = moved(normed, left)
    far_0 = moved(from_left[:half], right)
    far_1 = moved(from_right[half:], left)
    own_blocks = []
    away_blocks = []
    for tokens in ((normed,), (from_left,), (from_right,), (far_0, far_1)):
        both = tokens + tuple(moved(t, other_core) for t in tokens)
        own, away = project(parts, both, w_qkv, w_parts)
        own_blocks.append(own)
        away_blocks.append(moved(away, opposite_z))
    places = []
    for z_of in (z_high, 1 - z_high):
        for step in (0, 3, 1, 2):
            for core_of in (core, 1 - core):
                places.append((((x + step) % XS) * 2 + z_of) * 2 + core_of)
    place = jnp.stack(places).astype(jnp.int32)
    head_outputs = attention(place, own_blocks + away_blocks)

    attended = lax.all_to_all(head_outputs, "seq", split_axis=0, concat_axis=1, tiled=True)
    new_latent = update_rows(attended, noisy_latents[0], w_out)[None]

    slot_index = z_low * YS + y
    source = lax.dynamic_index_in_dim(queue, slot_index, 0, keepdims=False)
    limit = lax.dynamic_index_in_dim(frame_counts, source, 0, keepdims=False)
    others = new_latent
    others = jnp.concatenate(
        [others, moved(others, lambda x, y, z, core: (x, y, z ^ 1, core))], axis=0
    )
    others = jnp.concatenate(
        [others, moved(others, lambda x, y, z, core: (x, y ^ 1, z, core))], axis=0
    )
    others = jnp.concatenate(
        [others, moved(others, lambda x, y, z, core: (x, y ^ 2, z, core))], axis=0
    )
    apart = source ^ slot_index
    block = (apart // YS) + 2 * (apart % YS)
    chosen = lax.dynamic_index_in_dim(others, block, 0, keepdims=False)
    padded = padded_2(chosen, (("seq", 2),), 1)
    decoded = causal_features(padded, limit, conv_w, conv_b)
    return (attended[None], decoded[None])


def solution(mesh):
    return jax.shard_map(
        on_device,
        mesh=mesh,
        in_specs=(
            P(("group", "dp"), "seq", None),
            P(("group", "dp"), None, None),
            P(None, None, "seq"),
            P(),
            P(("group", "dp"), None, None, "seq", None),
            P(),
            P(),
            P(),
            P(),
        ),
        out_specs=(P(("group", "dp"), "seq", None), P(("group", "dp"), None, None, "seq", None)),
        check_vma=False,
    )
```

```python
import functools
import math

import jax
import jax.numpy as jnp
from jax import lax
from jax.experimental import pallas as pl
from jax.experimental.pallas import tpu as pltpu
from jax.sharding import PartitionSpec as P

HEAD_DIM = 128
EVERY = ("group", "seq", "dp")
XS, ZS, YS = (4, 4, 4)
VMEM_BYTES = 20 << 20
QUERY_SCALE = math.log2(math.e) / math.sqrt(HEAD_DIM)
NT = (((1,), (1,)), ((), ()))


def linear(x, y, z, core):
    return ((z % 2) * 16 + (x * 2 + z // 2) * 2 + core) * YS + y


def moved(array, move):
    perm = []
    for x in range(XS):
        for y in range(YS):
            for z in range(ZS):
                for core in range(2):
                    to = move(x, y, z, core)
                    there = linear(to[0] % XS, to[1] % YS, to[2] % ZS, to[3])
                    perm.append((linear(x, y, z, core), there))
    return lax.ppermute(array, EVERY, perm)


def right(x, y, z, core):
    return (x + 1, y, z, core)


def left(x, y, z, core):
    return (x - 1, y, z, core)


def other_core(x, y, z, core):
    return (x, y, z, 1 - core)


def opposite_z(x, y, z, core):
    return (x, y, z + 2, core)


def mirrored_z(x, y, z, core):
    return (x, y, 3 - z, core)


def project_kernel(n_tokens, part_ref, *refs):
    tokens = refs[:n_tokens]
    w_ref = refs[n_tokens]
    w_parts = refs[n_tokens + 1 : n_tokens + 5]
    own_ref, away_ref = refs[n_tokens + 5 :]
    for c in range(3):
        total = None
        for k in range(4):
            depth = w_parts[k].shape[1]
            at = pl.multiple_of(part_ref[k] * depth, depth)
            rows = jnp.concatenate([t[:, pl.ds(at, depth)] for t in tokens], axis=0)
            columns = jnp.concatenate([w_ref[c, pl.ds(at, depth), :], w_parts[k][c]], axis=1)
            term = jnp.dot(rows, columns, preferred_element_type=jnp.float32)
            total = term if total is None else total + term
        if c == 0:
            total = total * QUERY_SCALE
        total = total.astype(jnp.bfloat16)
        own_ref[c] = total[:, :HEAD_DIM]
        away_ref[c] = total[:, HEAD_DIM:]


def project(parts, tokens, w_qkv, w_parts):
    rows = sum(t.shape[0] for t in tokens)
    depth = w_qkv.shape[1]
    vmem = pl.BlockSpec(memory_space=pltpu.VMEM)
    out = jax.ShapeDtypeStruct((3, rows, HEAD_DIM), jnp.bfloat16)
    return pl.pallas_call(
        functools.partial(project_kernel, len(tokens)),
        in_specs=[pl.BlockSpec(memory_space=pltpu.SMEM)] + [vmem] * (len(tokens) + 5),
        out_specs=[vmem, vmem],
        out_shape=(out, out),
        compiler_params=pltpu.CompilerParams(vmem_limit_bytes=VMEM_BYTES),
        cost_estimate=pl.CostEstimate(
            flops=rows * depth * 6 * HEAD_DIM * 2,
            bytes_accessed=rows * depth * 2 + depth * 6 * HEAD_DIM * 2,
            transcendentals=0,
        ),
    )(parts, *tokens, w_qkv, *w_parts)


def attend(q, blocks, state, chunk=256):
    ones = jnp.ones((chunk, HEAD_DIM), jnp.bfloat16)
    for block in blocks:
        for at in range(0, block.shape[1], chunk):
            keys = block[1, at : at + chunk, :]
            vals = jnp.concatenate([block[2, at : at + chunk, :], ones], axis=1)
            scores = lax.dot_general(q, keys, NT, preferred_element_type=jnp.float32)
            high = jnp.max(scores, axis=1, keepdims=True)
            if state is not None:
                high = jnp.maximum(state[0], high)
            probs = jnp.exp2(scores - high).astype(jnp.bfloat16)
            term = jnp.dot(probs, vals, preferred_element_type=jnp.float32)
            if state is not None:
                term = state[1] * jnp.exp2(state[0] - high) + term
            state = (high, term)
    return state


def finished(state):
    total = state[1]
    return (total[:, :HEAD_DIM] / total[:, HEAD_DIM:]).astype(jnp.bfloat16)


def first_kernel(n_blocks, *refs):
    blocks = refs[:n_blocks]
    q_ref, top_ref, total_ref, q_all = refs[n_blocks:]

    @pl.when(pl.program_id(0) == 0)
    def _():
        for i, block in enumerate(blocks):
            q_all[i * block.shape[1] : (i + 1) * block.shape[1], :] = block[0]

    rows = q_ref.shape[0]
    q = q_all[pl.ds(pl.multiple_of(pl.program_id(0) * rows, rows), rows), :]
    top, total = attend(q, blocks, None)
    q_ref[...] = q
    top_ref[...] = jnp.broadcast_to(top, top_ref.shape)
    total_ref[...] = total


def last_kernel(n_blocks, tiles, place_ref, *refs):
    blocks = refs[:n_blocks]
    q_ref, top_ref, total_ref, out_ref = refs[n_blocks:]
    rows = blocks[0].shape[1]
    half = rows // 2
    step = half // 2

    def put(first, outputs):
        for at in range(0, outputs.shape[0], step):
            owner, inside = divmod(first + at, half)
            to = pl.multiple_of(place_ref[owner] * half + inside, step)
            out_ref[pl.ds(to, step), :] = outputs[at : at + step]

    known = q_ref.shape[0]
    tile = known // tiles
    for t in range(tiles):
        here = slice(t * tile, (t + 1) * tile)
        state = (top_ref[here, :][:, :1], total_ref[here, :])
        put(t * tile, finished(attend(q_ref[here, :], blocks[-1:], state)))
    put(known, finished(attend(blocks[-1][0], blocks, None)))


def attention(place, blocks):
    early = blocks[:-1]
    rows = blocks[0].shape[1]
    known = rows * len(early)
    tile = known // 4
    tokens = known + rows
    vmem = pl.BlockSpec(memory_space=pltpu.VMEM)

    def cost(queries, keys):
        return pl.CostEstimate(
            flops=queries * keys * HEAD_DIM * 4,
            bytes_accessed=tokens * HEAD_DIM * 8,
            transcendentals=queries * keys,
        )

    q, top, total = pl.pallas_call(
        functools.partial(first_kernel, len(early)),
        grid=(known // tile,),
        in_specs=[vmem] * len(early),
        out_specs=[
            pl.BlockSpec((tile, HEAD_DIM), lambda i: (i, 0)),
            pl.BlockSpec((tile, HEAD_DIM), lambda i: (i, 0)),
            pl.BlockSpec((tile, 2 * HEAD_DIM), lambda i: (i, 0)),
        ],
        out_shape=[
            jax.ShapeDtypeStruct((known, HEAD_DIM), jnp.bfloat16),
            jax.ShapeDtypeStruct((known, HEAD_DIM), jnp.float32),
            jax.ShapeDtypeStruct((known, 2 * HEAD_DIM), jnp.float32),
        ],
        scratch_shapes=[pltpu.VMEM((known, HEAD_DIM), jnp.bfloat16)],
        compiler_params=pltpu.CompilerParams(vmem_limit_bytes=VMEM_BYTES),
        cost_estimate=cost(known, known),
    )(*early)
    return pl.pallas_call(
        functools.partial(last_kernel, len(blocks), 4),
        in_specs=[pl.BlockSpec(memory_space=pltpu.SMEM)] + [vmem] * (len(blocks) + 3),
        out_specs=vmem,
        out_shape=jax.ShapeDtypeStruct((tokens, HEAD_DIM), jnp.bfloat16),
        compiler_params=pltpu.CompilerParams(vmem_limit_bytes=VMEM_BYTES),
        cost_estimate=cost(2 * rows, tokens),
    )(place, *blocks, q, top, total)


def update_kernel(att_ref, noisy_ref, w_ref, out_ref):
    heads, tokens, width = att_ref.shape
    squares = jnp.zeros((tokens, width), jnp.float32)
    for h in range(heads):
        values = att_ref[h].astype(jnp.float32)
        squares += values * values
    mean = jnp.sum(squares, axis=1, keepdims=True) / (heads * width)
    gain = lax.rsqrt(mean + 1e-06)
    predicted = jnp.zeros((w_ref.shape[0], tokens), jnp.float32)
    for h in range(heads):
        normed = (att_ref[h].astype(jnp.float32) * gain).astype(jnp.bfloat16)
        predicted += lax.dot_general(
            w_ref[:, h * width : (h + 1) * width], normed, NT, preferred_element_type=jnp.float32
        )
    half = predicted.shape[0] // 2
    both = jnp.concatenate([predicted[:half], predicted[half:]], axis=1)
    parts = []
    for _ in range(3):
        part = both.astype(jnp.bfloat16)
        both = both - part.astype(jnp.float32)
        parts.append(part)
    token = lax.broadcasted_iota(jnp.int32, (2 * tokens, 2 * tokens), 0)
    column = lax.broadcasted_iota(jnp.int32, (2 * tokens, 2 * tokens), 1)
    spread = jnp.where(token < tokens, 2 * token, 2 * token - 2 * tokens + 1) == column
    spread = jnp.where(spread, 1.0, 0.0).astype(jnp.bfloat16)
    grid = jnp.dot(jnp.concatenate(parts, axis=0), spread, preferred_element_type=jnp.float32)
    grid = grid[:half] + grid[half : 2 * half] + grid[2 * half :]
    channels = half // 2
    frames = 2 * tokens // 128
    for dy in range(2):
        for f in range(frames):
            at = (dy * frames + f) * channels
            rows = grid[dy * channels : (dy + 1) * channels, f * 128 : (f + 1) * 128]
            noisy = noisy_ref[at : at + channels, :].astype(jnp.float32)
            out_ref[at : at + channels, :] = (noisy + rows).astype(jnp.bfloat16)


def update_rows(by_head, noisy, w_out):
    channels, frames, rows, columns = noisy.shape
    noisy = noisy.transpose(2, 1, 0, 3).reshape(rows * frames * channels, columns)
    w_rows = w_out.T.reshape(channels, 2, 2, -1).transpose(2, 1, 0, 3).reshape(4 * channels, -1)
    return pl.pallas_call(
        update_kernel,
        in_specs=[pl.BlockSpec(memory_space=pltpu.VMEM)] * 3,
        out_specs=pl.BlockSpec(memory_space=pltpu.VMEM),
        out_shape=jax.ShapeDtypeStruct(noisy.shape, jnp.bfloat16),
        compiler_params=pltpu.CompilerParams(vmem_limit_bytes=VMEM_BYTES),
    )(by_head, noisy, w_rows)


def features_kernel(limit_ref, rows_ref, before_ref, after_ref, w_ref, b_ref, out_ref, taps):
    frames, channels = (4, 16)
    line = frames * channels
    four = jnp.concatenate([before_ref[...], rows_ref[...], after_ref[...]], axis=0)
    wide = four.astype(jnp.float32)
    lane = lax.broadcasted_iota(jnp.int32, wide.shape, 1)
    from_left = jnp.where(lane == 0, 0.0, pltpu.roll(wide, 1, 1)).astype(jnp.bfloat16)
    from_right = jnp.where(lane == 127, 0.0, pltpu.roll(wide, 127, 1)).astype(jnp.bfloat16)
    shifted = (from_left, four, from_right)
    for dt in range(3):
        for dh in range(3):
            for dw in range(3):
                tap = (dt * 3 + dh) * 3 + dw
                for f in range(frames):
                    for y in range(2):
                        at = (y + dh) * line + max(f + dt - 2, 0) * channels
                        block = (f * 2 + y) * 128
                        taps[tap * channels : (tap + 1) * channels, block : block + 128] = shifted[
                            dw
                        ][at : at + channels]
    features = lax.dot_general(
        w_ref[...], taps[...], (((0,), (0,)), ((), ())), preferred_element_type=jnp.float32
    )
    features = features + b_ref[...]
    frame = lax.broadcasted_iota(jnp.int32, features.shape, 1) // 256
    features = jnp.where(frame < limit_ref[0], features, 0.0)
    out_ref[...] = features.reshape(out_ref.shape).astype(jnp.bfloat16)


def causal_features(rows, before, after, limit, conv_w, conv_b):
    outputs, depth = conv_w.shape
    columns = rows.shape[1]
    vmem = pl.BlockSpec(memory_space=pltpu.VMEM)
    out = pl.pallas_call(
        features_kernel,
        in_specs=[pl.BlockSpec(memory_space=pltpu.SMEM)] + [vmem] * 5,
        out_specs=vmem,
        out_shape=jax.ShapeDtypeStruct((outputs, 8, columns), jnp.bfloat16),
        scratch_shapes=[pltpu.VMEM((depth, 8 * columns), jnp.bfloat16)],
        compiler_params=pltpu.CompilerParams(vmem_limit_bytes=VMEM_BYTES),
    )(limit[None], rows, before, after, conv_w.T, conv_b[:, None])
    return out.reshape(outputs, 4, 2, columns)


def on_device(
    latent_tokens, modulation, w_qkv, w_out, noisy_latents, queue, frame_counts, conv_w, conv_b
):
    z_low = lax.axis_index("group")
    seat = lax.axis_index("seq")
    y = lax.axis_index("dp")
    x, z_high, core = (seat // 4, seat // 2 % 2, seat % 2)

    quarter = w_qkv.shape[1] // 4
    part_0 = moved(lax.dynamic_slice_in_dim(w_qkv, y * quarter, quarter, axis=1), mirrored_z)
    part_2 = lax.dynamic_slice_in_dim(w_qkv, (y + 2) % 4 * quarter, quarter, axis=1)
    parts = (y + jnp.arange(4, dtype=jnp.int32)) % 4

    values = latent_tokens[0].astype(jnp.float32)
    shift_scale = modulation[0]
    scaled = values * lax.rsqrt(jnp.mean(values * values, axis=-1, keepdims=True) + 1e-06)
    normed = (scaled * (1.0 + shift_scale[1]) + shift_scale[0]).astype(jnp.bfloat16)

    half = normed.shape[0] // 2
    from_left = moved(normed, right)
    from_right = moved(normed, left)
    swapped = moved(normed, other_core)
    part_0, part_2, swapped = lax.optimization_barrier((part_0, part_2, swapped))
    part_1 = moved(part_0, lambda x, y, z, core: (x, y - 1, z, core))
    part_3 = moved(part_0, lambda x, y, z, core: (x, y + 1, z, core))
    part_2 = moved(part_2, mirrored_z)
    from_left, from_right, part_1, part_2, part_3 = lax.optimization_barrier(
        (from_left, from_right, part_1, part_2, part_3)
    )
    w_parts = (part_0, part_1, part_2, part_3)

    def projected(*both):
        own, away = project(parts, both, w_qkv, w_parts)
        return own, moved(away, opposite_z)

    far_0 = moved(from_left[:half], right)
    far_1 = moved(from_right[half:], left)
    blocks = [projected(normed, swapped)]
    blocks.append(projected(from_left, moved(from_left, other_core)))
    blocks.append(projected(from_right, moved(from_right, other_core)))
    far_0, far_1, blocks[0], blocks[1], own = lax.optimization_barrier(
        (far_0, far_1, blocks[0], blocks[1], blocks[2][0])
    )
    blocks[2] = (own, blocks[2][1])
    blocks.append(projected(far_0, far_1, moved(far_0, other_core), moved(far_1, other_core)))
    places = []
    for z_of in (z_high, 1 - z_high):
        for step in (0, 3, 1, 2):
            for core_of in (core, 1 - core):
                places.append((((x + step) % XS) * 2 + z_of) * 2 + core_of)
    place = jnp.stack(places).astype(jnp.int32)
    head_outputs = attention(place, [b[0] for b in blocks] + [b[1] for b in blocks])

    tokens = latent_tokens.shape[1]
    by_head = lax.all_to_all(
        head_outputs.reshape(-1, tokens, HEAD_DIM), "seq", split_axis=0, concat_axis=0, tiled=True
    )
    attended = by_head.transpose(1, 0, 2).reshape(1, tokens, -1)
    new_rows = update_rows(by_head, noisy_latents[0], w_out)

    slot_index = z_low * YS + y
    source = lax.dynamic_index_in_dim(queue, slot_index, 0, keepdims=False)
    limit = lax.dynamic_index_in_dim(frame_counts, source, 0, keepdims=False)
    everyone = lax.all_to_all(
        jnp.broadcast_to(new_rows, (2 * YS,) + new_rows.shape),
        ("group", "dp"),
        split_axis=0,
        concat_axis=0,
        tiled=True,
    )
    chosen = lax.dynamic_index_in_dim(everyone, source, 0, keepdims=False)
    line = chosen.shape[0] // 2
    seats = lax.axis_size("seq")
    up = [(i, i + 1) for i in range(seats - 1)]
    before = lax.ppermute(chosen[line:], "seq", up)
    after = lax.ppermute(chosen[:line], "seq", [(j, i) for i, j in up])
    decoded = causal_features(chosen, before, after, limit, conv_w, conv_b)
    return (attended, decoded[None])


def solution(mesh):
    return jax.shard_map(
        on_device,
        mesh=mesh,
        in_specs=(
            P(("group", "dp"), "seq", None),
            P(("group", "dp"), None, None),
            P(None, None, "seq"),
            P(),
            P(("group", "dp"), None, None, "seq", None),
            P(),
            P(),
            P(),
            P(),
        ),
        out_specs=(P(("group", "dp"), "seq", None), P(("group", "dp"), None, None, "seq", None)),
        check_vma=False,
    )
```

```python
import functools
import math

import jax
import jax.numpy as jnp
from jax import lax
from jax.experimental import pallas as pl
from jax.experimental.pallas import tpu as pltpu
from jax.sharding import PartitionSpec as P

HEAD_DIM = 128
EVERY = ("group", "seq", "dp")
XS, ZS, YS = (4, 4, 4)
VMEM_BYTES = 12 << 20
QUERY_SCALE = math.log2(math.e) / math.sqrt(HEAD_DIM)
TINY = pl.CostEstimate(flops=1, bytes_accessed=1, transcendentals=0)
NT = (((1,), (1,)), ((), ()))


def linear(x, y, z, core):
    return ((z % 2) * 16 + (x * 2 + z // 2) * 2 + core) * YS + y


def moved(array, move):
    perm = []
    for x in range(XS):
        for y in range(YS):
            for z in range(ZS):
                for core in range(2):
                    to = move(x, y, z, core)
                    there = linear(to[0] % XS, to[1] % YS, to[2] % ZS, to[3])
                    perm.append((linear(x, y, z, core), there))
    return lax.ppermute(array, EVERY, perm)


def right(x, y, z, core):
    return (x + 1, y, z, core)


def left(x, y, z, core):
    return (x - 1, y, z, core)


def other_core(x, y, z, core):
    return (x, y, z, 1 - core)


def opposite_z(x, y, z, core):
    return (x, y, z + 2, core)


def mirrored_z(x, y, z, core):
    return (x, y, 3 - z, core)


def project_kernel(n_tokens, part_ref, *refs):
    tokens = refs[:n_tokens]
    w_ref = refs[n_tokens]
    w_parts = refs[n_tokens + 1 : n_tokens + 5]
    own_ref, away_ref = refs[n_tokens + 5 :]
    for c in range(3):
        total = None
        for k in range(4):
            depth = w_parts[k].shape[1]
            at = pl.multiple_of(part_ref[k] * depth, depth)
            rows = jnp.concatenate([t[:, pl.ds(at, depth)] for t in tokens], axis=0)
            columns = jnp.concatenate([w_ref[c, pl.ds(at, depth), :], w_parts[k][c]], axis=1)
            term = jnp.dot(rows, columns, preferred_element_type=jnp.float32)
            total = term if total is None else total + term
        if c == 0:
            total = total * QUERY_SCALE
        total = total.astype(jnp.bfloat16)
        own_ref[c] = total[:, :HEAD_DIM]
        away_ref[c] = total[:, HEAD_DIM:]


def project(parts, tokens, w_qkv, w_parts):
    rows = sum(t.shape[0] for t in tokens)
    depth = w_qkv.shape[1]
    vmem = pl.BlockSpec(memory_space=pltpu.VMEM)
    out = jax.ShapeDtypeStruct((3, rows, HEAD_DIM), jnp.bfloat16)
    return pl.pallas_call(
        functools.partial(project_kernel, len(tokens)),
        in_specs=[pl.BlockSpec(memory_space=pltpu.SMEM)] + [vmem] * (len(tokens) + 5),
        out_specs=[vmem, vmem],
        out_shape=(out, out),
        compiler_params=pltpu.CompilerParams(vmem_limit_bytes=VMEM_BYTES),
        cost_estimate=TINY,
    )(parts, *tokens, w_qkv, *w_parts)


def attend(q, blocks, state, chunk=256):
    ones = jnp.ones((chunk, HEAD_DIM), jnp.bfloat16)
    for block in blocks:
        for at in range(0, block.shape[1], chunk):
            keys = block[1, at : at + chunk, :]
            vals = jnp.concatenate([block[2, at : at + chunk, :], ones], axis=1)
            scores = lax.dot_general(q, keys, NT, preferred_element_type=jnp.float32)
            high = jnp.max(scores, axis=1, keepdims=True)
            if state is not None:
                high = jnp.maximum(state[0], high)
            probs = jnp.exp2(scores - high).astype(jnp.bfloat16)
            term = jnp.dot(probs, vals, preferred_element_type=jnp.float32)
            if state is not None:
                term = state[1] * jnp.exp2(state[0] - high) + term
            state = (high, term)
    return state


def finished(state):
    total = state[1]
    return (total[:, :HEAD_DIM] / total[:, HEAD_DIM:]).astype(jnp.bfloat16)


def phase_kernel(n_old, n_new, last, place_ref, *refs):
    rows = refs[0].shape[1]

    def cut(group):
        return [b.at[:, i : i + rows, :] for b in group for i in range(0, b.shape[1], rows)]

    old = cut(refs[:n_old])
    new = cut(refs[n_old : n_old + n_new])
    refs = refs[n_old + n_new :]
    blocks = old + new
    n_old = len(old)
    n_new = len(new)
    run = rows // 2
    if n_old:
        top_ref, total_ref = refs[:2]
        refs = refs[2:]

    def put(first, state):
        for i in range(state[1].shape[0] // rows):
            here = slice(i * rows, (i + 1) * rows)
            if last:
                outputs = finished((state[0][here], state[1][here]))
                for j in range(2):
                    at = pl.multiple_of(place_ref[2 * (first + i) + j] * run, run)
                    refs[0][pl.ds(at, run), :] = outputs[j * run : (j + 1) * run]
            else:
                there = slice((first + i) * rows, (first + i + 1) * rows)
                refs[0][there, :] = jnp.broadcast_to(state[0][here], (rows, HEAD_DIM))
                refs[1][there, :] = state[1][here]

    def queries(group):
        return jnp.concatenate([b[0] for b in group], axis=0)

    for first in range(0, n_old, 2):
        group = old[first : first + 2]
        here = slice(first * rows, (first + len(group)) * rows)
        state = (jnp.max(top_ref[here, :], axis=1, keepdims=True), total_ref[here, :])
        put(first, attend(queries(group), new, state))
    for first in range(0, n_new, 2):
        group = new[first : first + 2]
        put(n_old + first, attend(queries(group), blocks, None))


def phase(place, old, new, state, last):
    blocks = list(old) + list(new)
    tokens = sum(b.shape[1] for b in blocks)
    vmem = pl.BlockSpec(memory_space=pltpu.VMEM)
    if last:
        out_shape = [jax.ShapeDtypeStruct((tokens, HEAD_DIM), jnp.bfloat16)]
    else:
        out_shape = [
            jax.ShapeDtypeStruct((tokens, HEAD_DIM), jnp.float32),
            jax.ShapeDtypeStruct((tokens, 2 * HEAD_DIM), jnp.float32),
        ]
    return pl.pallas_call(
        functools.partial(phase_kernel, len(old), len(new), last),
        in_specs=[pl.BlockSpec(memory_space=pltpu.SMEM)] + [vmem] * (len(blocks) + len(state)),
        out_specs=[vmem] * len(out_shape),
        out_shape=out_shape,
        compiler_params=pltpu.CompilerParams(vmem_limit_bytes=VMEM_BYTES),
        cost_estimate=TINY,
    )(place, *blocks, *state)


def update_kernel(att_ref, noisy_ref, w_ref, out_ref):
    heads, tokens, width = att_ref.shape
    squares = jnp.zeros((tokens, width), jnp.float32)
    for h in range(heads):
        values = att_ref[h].astype(jnp.float32)
        squares += values * values
    mean = jnp.sum(squares, axis=1, keepdims=True) / (heads * width)
    gain = lax.rsqrt(mean + 1e-06)
    predicted = jnp.zeros((w_ref.shape[0], tokens), jnp.float32)
    for h in range(heads):
        normed = (att_ref[h].astype(jnp.float32) * gain).astype(jnp.bfloat16)
        predicted += lax.dot_general(
            w_ref[:, h * width : (h + 1) * width], normed, NT, preferred_element_type=jnp.float32
        )
    half = predicted.shape[0] // 2
    both = jnp.concatenate([predicted[:half], predicted[half:]], axis=1)
    parts = []
    for _ in range(3):
        part = both.astype(jnp.bfloat16)
        both = both - part.astype(jnp.float32)
        parts.append(part)
    token = lax.broadcasted_iota(jnp.int32, (2 * tokens, 2 * tokens), 0)
    column = lax.broadcasted_iota(jnp.int32, (2 * tokens, 2 * tokens), 1)
    spread = jnp.where(token < tokens, 2 * token, 2 * token - 2 * tokens + 1) == column
    spread = jnp.where(spread, 1.0, 0.0).astype(jnp.bfloat16)
    grid = jnp.dot(jnp.concatenate(parts, axis=0), spread, preferred_element_type=jnp.float32)
    grid = grid[:half] + grid[half : 2 * half] + grid[2 * half :]
    channels = half // 2
    frames = 2 * tokens // 128
    for dy in range(2):
        for f in range(frames):
            at = (dy * frames + f) * channels
            rows = grid[dy * channels : (dy + 1) * channels, f * 128 : (f + 1) * 128]
            noisy = noisy_ref[at : at + channels, :].astype(jnp.float32)
            updated = (noisy + rows).astype(jnp.bfloat16)
            for i in range(out_ref.shape[0]):
                out_ref[i, at : at + channels, :] = updated


def update_rows(by_head, noisy, w_out, copies):
    channels, frames, rows, columns = noisy.shape
    noisy = noisy.transpose(2, 1, 0, 3).reshape(rows * frames * channels, columns)
    w_rows = w_out.T.reshape(channels, 2, 2, -1).transpose(2, 1, 0, 3).reshape(4 * channels, -1)
    return pl.pallas_call(
        update_kernel,
        in_specs=[pl.BlockSpec(memory_space=pltpu.VMEM)] * 3,
        out_specs=pl.BlockSpec(memory_space=pltpu.VMEM),
        out_shape=jax.ShapeDtypeStruct((copies,) + noisy.shape, jnp.bfloat16),
        compiler_params=pltpu.CompilerParams(vmem_limit_bytes=VMEM_BYTES),
        cost_estimate=TINY,
    )(by_head, noisy, w_rows)


def features_kernel(limit_ref, rows_ref, before_ref, after_ref, w_ref, b_ref, out_ref, taps):
    frames, channels = (4, 16)
    line = frames * channels
    four = jnp.concatenate([before_ref[...], rows_ref[...], after_ref[...]], axis=0)
    wide = four.astype(jnp.float32)
    lane = lax.broadcasted_iota(jnp.int32, wide.shape, 1)
    from_left = jnp.where(lane == 0, 0.0, pltpu.roll(wide, 1, 1)).astype(jnp.bfloat16)
    from_right = jnp.where(lane == 127, 0.0, pltpu.roll(wide, 127, 1)).astype(jnp.bfloat16)
    shifted = (from_left, four, from_right)
    for dt in range(3):
        for dh in range(3):
            for dw in range(3):
                tap = (dt * 3 + dh) * 3 + dw
                for f in range(frames):
                    for y in range(2):
                        at = (y + dh) * line + max(f + dt - 2, 0) * channels
                        block = (f * 2 + y) * 128
                        taps[tap * channels : (tap + 1) * channels, block : block + 128] = shifted[
                            dw
                        ][at : at + channels]
    features = lax.dot_general(
        w_ref[...], taps[...], (((0,), (0,)), ((), ())), preferred_element_type=jnp.float32
    )
    features = features + b_ref[...]
    frame = lax.broadcasted_iota(jnp.int32, features.shape, 1) // 256
    features = jnp.where(frame < limit_ref[0], features, 0.0)
    out_ref[...] = features.reshape(out_ref.shape).astype(jnp.bfloat16)


def causal_features(rows, before, after, limit, conv_w, conv_b):
    outputs, depth = conv_w.shape
    columns = rows.shape[1]
    vmem = pl.BlockSpec(memory_space=pltpu.VMEM)
    out = pl.pallas_call(
        features_kernel,
        in_specs=[pl.BlockSpec(memory_space=pltpu.SMEM)] + [vmem] * 5,
        out_specs=vmem,
        out_shape=jax.ShapeDtypeStruct((outputs, 8, columns), jnp.bfloat16),
        scratch_shapes=[pltpu.VMEM((depth, 8 * columns), jnp.bfloat16)],
        compiler_params=pltpu.CompilerParams(vmem_limit_bytes=VMEM_BYTES),
        cost_estimate=TINY,
    )(limit[None], rows, before, after, conv_w.T, conv_b[:, None])
    return out.reshape(outputs, 4, 2, columns)


def on_device(
    latent_tokens, modulation, w_qkv, w_out, noisy_latents, queue, frame_counts, conv_w, conv_b
):
    z_low = lax.axis_index("group")
    seat = lax.axis_index("seq")
    y = lax.axis_index("dp")
    x, z_high, core = (seat // 4, seat // 2 % 2, seat % 2)

    quarter = w_qkv.shape[1] // 4
    part_0 = moved(lax.dynamic_slice_in_dim(w_qkv, y * quarter, quarter, axis=1), mirrored_z)
    part_2 = lax.dynamic_slice_in_dim(w_qkv, (y + 2) % 4 * quarter, quarter, axis=1)
    parts = (y + jnp.arange(4, dtype=jnp.int32)) % 4

    values = latent_tokens[0].astype(jnp.float32)
    shift_scale = modulation[0]
    scaled = values * lax.rsqrt(jnp.mean(values * values, axis=-1, keepdims=True) + 1e-06)
    normed = (scaled * (1.0 + shift_scale[1]) + shift_scale[0]).astype(jnp.bfloat16)

    half = normed.shape[0] // 2
    from_left = moved(normed, right)
    from_right = moved(normed, left)
    swapped = moved(normed, other_core)
    part_0, part_2, swapped = lax.optimization_barrier((part_0, part_2, swapped))
    part_1 = moved(part_0, lambda x, y, z, core: (x, y - 1, z, core))
    part_3 = moved(part_0, lambda x, y, z, core: (x, y + 1, z, core))
    part_2 = moved(part_2, mirrored_z)
    from_left, from_right, part_1, part_2, part_3 = lax.optimization_barrier(
        (from_left, from_right, part_1, part_2, part_3)
    )
    w_parts = (part_0, part_1, part_2, part_3)

    def projected(*both):
        own, away = project(parts, both, w_qkv, w_parts)
        return own, moved(away, opposite_z)

    far_0 = moved(from_left[:half], right)
    far_1 = moved(from_right[half:], left)
    own_0, away_0 = projected(normed, swapped)
    own_1, away_1 = projected(from_left, moved(from_left, other_core))
    own_2, away_2 = projected(from_right, moved(from_right, other_core))
    far_0, far_1, away_0, own_1, own_2 = lax.optimization_barrier(
        (far_0, far_1, away_0, own_1, own_2)
    )
    both = (far_0, far_1, moved(far_0, other_core), moved(far_1, other_core))
    own_3, away_3 = project(parts, both, w_qkv, w_parts)

    places = []
    early = [own_0, own_1, own_2, own_3, away_0]
    for step, z_of in zip((0, 3, 1, 2, 0, 3, 1, 2), (z_high,) * 4 + (1 - z_high,) * 4):
        for core_of in (core, 1 - core):
            places.append((((x + step) % XS) * 2 + z_of) * 2 + core_of)
    place = jnp.stack(places).astype(jnp.int32)
    state = phase(place, [], early, [], False)
    away_3, state = lax.optimization_barrier((away_3, state))
    away_3 = moved(away_3, opposite_z)
    state = phase(place, early, [away_1, away_2], state, False)
    (head_outputs,) = phase(place, early + [away_1, away_2], [away_3], state, True)

    tokens = latent_tokens.shape[1]
    by_head = lax.all_to_all(
        head_outputs.reshape(-1, tokens, HEAD_DIM), "seq", split_axis=0, concat_axis=0, tiled=True
    )
    attended = by_head.transpose(1, 0, 2).reshape(1, tokens, -1)
    new_rows = update_rows(by_head, noisy_latents[0], w_out, 2 * YS)

    slot_index = z_low * YS + y
    source = lax.dynamic_index_in_dim(queue, slot_index, 0, keepdims=False)
    limit = lax.dynamic_index_in_dim(frame_counts, source, 0, keepdims=False)
    everyone = lax.all_to_all(
        new_rows, ("group", "dp"), split_axis=0, concat_axis=0, tiled=True
    )
    chosen = lax.dynamic_index_in_dim(everyone, source, 0, keepdims=False)
    line = chosen.shape[0] // 2
    seats = lax.axis_size("seq")
    up = [(i, i + 1) for i in range(seats - 1)]
    before = lax.ppermute(chosen[line:], "seq", up)
    after = lax.ppermute(chosen[:line], "seq", [(j, i) for i, j in up])
    decoded = causal_features(chosen, before, after, limit, conv_w, conv_b)
    return (attended, decoded[None])


def solution(mesh):
    return jax.shard_map(
        on_device,
        mesh=mesh,
        in_specs=(
            P(("group", "dp"), "seq", None),
            P(("group", "dp"), None, None),
            P(None, None, "seq"),
            P(),
            P(("group", "dp"), None, None, "seq", None),
            P(),
            P(),
            P(),
            P(),
        ),
        out_specs=(P(("group", "dp"), "seq", None), P(("group", "dp"), None, None, "seq", None)),
        check_vma=False,
    )
```

```python
import functools
import math

import jax
import jax.numpy as jnp
from jax import lax
from jax.experimental import pallas as pl
from jax.experimental.pallas import tpu as pltpu
from jax.sharding import PartitionSpec as P

HEAD_DIM = 128
EVERY = ("group", "seq", "dp")
XS, ZS, YS = (4, 4, 4)
VMEM_BYTES = 12 << 20
QUERY_SCALE = math.log2(math.e) / math.sqrt(HEAD_DIM)
TINY = pl.CostEstimate(flops=1, bytes_accessed=1, transcendentals=0)
NT = (((1,), (1,)), ((), ()))


def linear(x, y, z, core):
    return ((z % 2) * 16 + (x * 2 + z // 2) * 2 + core) * YS + y


def moved(array, move):
    perm = []
    for x in range(XS):
        for y in range(YS):
            for z in range(ZS):
                for core in range(2):
                    to = move(x, y, z, core)
                    there = linear(to[0] % XS, to[1] % YS, to[2] % ZS, to[3])
                    perm.append((linear(x, y, z, core), there))
    return lax.ppermute(array, EVERY, perm)


def right(x, y, z, core):
    return (x + 1, y, z, core)


def left(x, y, z, core):
    return (x - 1, y, z, core)


def other_core(x, y, z, core):
    return (x, y, z, 1 - core)


def opposite_z(x, y, z, core):
    return (x, y, z + 2, core)


def mirrored_z(x, y, z, core):
    return (x, y, 3 - z, core)


def project_kernel(n_tokens, part_ref, *refs):
    tokens = refs[:n_tokens]
    w_ref = refs[n_tokens]
    w_parts = refs[n_tokens + 1 : n_tokens + 5]
    own_ref, away_ref = refs[n_tokens + 5 :]

    def step(c, carry):
        total = None
        for k in range(4):
            depth = w_parts[k].shape[1]
            at = pl.multiple_of(part_ref[k] * depth, depth)
            rows = jnp.concatenate([t[:, pl.ds(at, depth)] for t in tokens], axis=0)
            columns = jnp.concatenate([w_ref[c, pl.ds(at, depth), :], w_parts[k][c]], axis=1)
            term = jnp.dot(rows, columns, preferred_element_type=jnp.float32)
            total = term if total is None else total + term
        total = (total * jnp.where(c == 0, QUERY_SCALE, 1.0)).astype(jnp.bfloat16)
        own_ref[c] = total[:, :HEAD_DIM]
        away_ref[c] = total[:, HEAD_DIM:]
        return carry

    lax.fori_loop(0, w_ref.shape[0], step, 0)


def project(parts, tokens, w_qkv, w_parts):
    rows = sum(t.shape[0] for t in tokens)
    depth = w_qkv.shape[1]
    vmem = pl.BlockSpec(memory_space=pltpu.VMEM)
    out = jax.ShapeDtypeStruct((3, rows, HEAD_DIM), jnp.bfloat16)
    return pl.pallas_call(
        functools.partial(project_kernel, len(tokens)),
        in_specs=[pl.BlockSpec(memory_space=pltpu.SMEM)] + [vmem] * (len(tokens) + 5),
        out_specs=[vmem, vmem],
        out_shape=(out, out),
        compiler_params=pltpu.CompilerParams(vmem_limit_bytes=VMEM_BYTES),
        cost_estimate=TINY,
    )(parts, *tokens, w_qkv, *w_parts)


def attend(q, blocks, state, chunk=256):
    ones = jnp.ones((chunk, HEAD_DIM), jnp.bfloat16)
    for block in blocks:
        for at in range(0, block.shape[1], chunk):
            keys = block[1, at : at + chunk, :]
            vals = jnp.concatenate([block[2, at : at + chunk, :], ones], axis=1)
            scores = lax.dot_general(q, keys, NT, preferred_element_type=jnp.float32)
            high = jnp.max(scores, axis=1, keepdims=True)
            if state is not None:
                high = jnp.maximum(state[0], high)
            probs = jnp.exp2(scores - high).astype(jnp.bfloat16)
            term = jnp.dot(probs, vals, preferred_element_type=jnp.float32)
            if state is not None:
                term = state[1] * jnp.exp2(state[0] - high) + term
            state = (high, term)
    return state


def finished(state):
    total = state[1]
    return (total[:, :HEAD_DIM] / total[:, HEAD_DIM:]).astype(jnp.bfloat16)


def phase_kernel(n_old, n_new, last, place_ref, *refs):
    old = refs[:n_old]
    new = refs[n_old : n_old + n_new]
    refs = refs[n_old + n_new :]
    q_all = refs[-1]
    rows = new[0].shape[1]
    for i, block in enumerate(old + new):
        q_all[i * rows : (i + 1) * rows, :] = block[0]
    owned = rows // 2
    run = owned // 2
    if n_old:
        top_ref, total_ref = refs[:2]
        refs = refs[2:]

    def put(at, state):
        size = state[1].shape[0]
        if last:
            outputs = finished(state)
            for i in range(size // run):
                piece = at // run + i
                to = place_ref[piece // 2] * owned + piece % 2 * run
                here = pl.ds(pl.multiple_of(to, run), run)
                refs[0][here, :] = outputs[i * run : (i + 1) * run]
        else:
            refs[0][pl.ds(at, size), :] = jnp.broadcast_to(state[0], (size, HEAD_DIM))
            refs[1][pl.ds(at, size), :] = state[1]

    def sweep(first, count, blocks, resumed):
        tiles = next(t for t in (1, 2, 4, 8) if count * rows // t <= 1280)
        size = count * rows // tiles

        def step(t, carry):
            at = pl.multiple_of(first * rows + t * size, run)
            here = pl.ds(at, size)
            state = None
            if resumed:
                state = (jnp.max(top_ref[here, :], axis=1, keepdims=True), total_ref[here, :])
            put(at, attend(q_all[here, :], blocks, state))
            return carry

        lax.fori_loop(0, tiles, step, 0)

    if n_old:
        sweep(0, n_old, new, True)
    sweep(n_old, n_new, old + new, False)


def phase(place, old, new, state, last):
    blocks = list(old) + list(new)
    tokens = sum(b.shape[1] for b in blocks)
    vmem = pl.BlockSpec(memory_space=pltpu.VMEM)
    if last:
        out_shape = [jax.ShapeDtypeStruct((tokens, HEAD_DIM), jnp.bfloat16)]
    else:
        out_shape = [
            jax.ShapeDtypeStruct((tokens, HEAD_DIM), jnp.float32),
            jax.ShapeDtypeStruct((tokens, 2 * HEAD_DIM), jnp.float32),
        ]
    return pl.pallas_call(
        functools.partial(phase_kernel, len(old), len(new), last),
        in_specs=[pl.BlockSpec(memory_space=pltpu.SMEM)] + [vmem] * (len(blocks) + len(state)),
        out_specs=[vmem] * len(out_shape),
        out_shape=out_shape,
        scratch_shapes=[pltpu.VMEM((tokens, HEAD_DIM), jnp.bfloat16)],
        compiler_params=pltpu.CompilerParams(vmem_limit_bytes=VMEM_BYTES),
        cost_estimate=TINY,
    )(place, *blocks, *state)


def update_kernel(att_ref, noisy_ref, w_ref, out_ref):
    heads, tokens, width = att_ref.shape
    squares = jnp.zeros((tokens, width), jnp.float32)
    for h in range(heads):
        values = att_ref[h].astype(jnp.float32)
        squares += values * values
    mean = jnp.sum(squares, axis=1, keepdims=True) / (heads * width)
    gain = lax.rsqrt(mean + 1e-06)
    predicted = jnp.zeros((w_ref.shape[0], tokens), jnp.float32)
    for h in range(heads):
        normed = (att_ref[h].astype(jnp.float32) * gain).astype(jnp.bfloat16)
        predicted += lax.dot_general(
            w_ref[:, h * width : (h + 1) * width], normed, NT, preferred_element_type=jnp.float32
        )
    half = predicted.shape[0] // 2
    both = jnp.concatenate([predicted[:half], predicted[half:]], axis=1)
    parts = []
    for _ in range(3):
        part = both.astype(jnp.bfloat16)
        both = both - part.astype(jnp.float32)
        parts.append(part)
    token = lax.broadcasted_iota(jnp.int32, (2 * tokens, 2 * tokens), 0)
    column = lax.broadcasted_iota(jnp.int32, (2 * tokens, 2 * tokens), 1)
    spread = jnp.where(token < tokens, 2 * token, 2 * token - 2 * tokens + 1) == column
    spread = jnp.where(spread, 1.0, 0.0).astype(jnp.bfloat16)
    grid = jnp.dot(jnp.concatenate(parts, axis=0), spread, preferred_element_type=jnp.float32)
    grid = grid[:half] + grid[half : 2 * half] + grid[2 * half :]
    channels = half // 2
    frames = 2 * tokens // 128
    for dy in range(2):
        for f in range(frames):
            at = (dy * frames + f) * channels
            rows = grid[dy * channels : (dy + 1) * channels, f * 128 : (f + 1) * 128]
            noisy = noisy_ref[at : at + channels, :].astype(jnp.float32)
            updated = (noisy + rows).astype(jnp.bfloat16)
            for i in range(out_ref.shape[0]):
                out_ref[i, at : at + channels, :] = updated


def update_rows(by_head, noisy, w_out, copies):
    channels, frames, rows, columns = noisy.shape
    noisy = noisy.transpose(2, 1, 0, 3).reshape(rows * frames * channels, columns)
    w_rows = w_out.T.reshape(channels, 2, 2, -1).transpose(2, 1, 0, 3).reshape(4 * channels, -1)
    return pl.pallas_call(
        update_kernel,
        in_specs=[pl.BlockSpec(memory_space=pltpu.VMEM)] * 3,
        out_specs=pl.BlockSpec(memory_space=pltpu.VMEM),
        out_shape=jax.ShapeDtypeStruct((copies,) + noisy.shape, jnp.bfloat16),
        compiler_params=pltpu.CompilerParams(vmem_limit_bytes=VMEM_BYTES),
        cost_estimate=TINY,
    )(by_head, noisy, w_rows)


def features_kernel(limit_ref, rows_ref, before_ref, after_ref, w_ref, b_ref, out_ref, taps):
    frames, channels = (4, 16)
    line = frames * channels
    four = jnp.concatenate([before_ref[...], rows_ref[...], after_ref[...]], axis=0)
    wide = four.astype(jnp.float32)
    lane = lax.broadcasted_iota(jnp.int32, wide.shape, 1)
    from_left = jnp.where(lane == 0, 0.0, pltpu.roll(wide, 1, 1)).astype(jnp.bfloat16)
    from_right = jnp.where(lane == 127, 0.0, pltpu.roll(wide, 127, 1)).astype(jnp.bfloat16)
    shifted = (from_left, four, from_right)
    for dt in range(3):
        for dh in range(3):
            for dw in range(3):
                tap = (dt * 3 + dh) * 3 + dw
                for f in range(frames):
                    for y in range(2):
                        at = (y + dh) * line + max(f + dt - 2, 0) * channels
                        block = (f * 2 + y) * 128
                        taps[tap * channels : (tap + 1) * channels, block : block + 128] = shifted[
                            dw
                        ][at : at + channels]
    features = lax.dot_general(
        w_ref[...], taps[...], (((0,), (0,)), ((), ())), preferred_element_type=jnp.float32
    )
    features = features + b_ref[...]
    frame = lax.broadcasted_iota(jnp.int32, features.shape, 1) // 256
    features = jnp.where(frame < limit_ref[0], features, 0.0)
    out_ref[...] = features.reshape(out_ref.shape).astype(jnp.bfloat16)


def causal_features(rows, before, after, limit, conv_w, conv_b):
    outputs, depth = conv_w.shape
    columns = rows.shape[1]
    vmem = pl.BlockSpec(memory_space=pltpu.VMEM)
    out = pl.pallas_call(
        features_kernel,
        in_specs=[pl.BlockSpec(memory_space=pltpu.SMEM)] + [vmem] * 5,
        out_specs=vmem,
        out_shape=jax.ShapeDtypeStruct((outputs, 8, columns), jnp.bfloat16),
        scratch_shapes=[pltpu.VMEM((depth, 8 * columns), jnp.bfloat16)],
        compiler_params=pltpu.CompilerParams(vmem_limit_bytes=VMEM_BYTES),
        cost_estimate=TINY,
    )(limit[None], rows, before, after, conv_w.T, conv_b[:, None])
    return out.reshape(outputs, 4, 2, columns)


def on_device(
    latent_tokens, modulation, w_qkv, w_out, noisy_latents, queue, frame_counts, conv_w, conv_b
):
    z_low = lax.axis_index("group")
    seat = lax.axis_index("seq")
    y = lax.axis_index("dp")
    x, z_high, core = (seat // 4, seat // 2 % 2, seat % 2)

    quarter = w_qkv.shape[1] // 4
    part_0 = moved(lax.dynamic_slice_in_dim(w_qkv, y * quarter, quarter, axis=1), mirrored_z)
    part_2 = lax.dynamic_slice_in_dim(w_qkv, (y + 2) % 4 * quarter, quarter, axis=1)
    parts = (y + jnp.arange(4, dtype=jnp.int32)) % 4

    values = latent_tokens[0].astype(jnp.float32)
    shift_scale = modulation[0]
    scaled = values * lax.rsqrt(jnp.mean(values * values, axis=-1, keepdims=True) + 1e-06)
    normed = (scaled * (1.0 + shift_scale[1]) + shift_scale[0]).astype(jnp.bfloat16)

    half = normed.shape[0] // 2
    from_left = moved(normed, right)
    from_right = moved(normed, left)
    swapped = moved(normed, other_core)
    part_0, part_2, swapped = lax.optimization_barrier((part_0, part_2, swapped))
    part_1 = moved(part_0, lambda x, y, z, core: (x, y - 1, z, core))
    part_3 = moved(part_0, lambda x, y, z, core: (x, y + 1, z, core))
    part_2 = moved(part_2, mirrored_z)
    from_left, from_right, part_1, part_2, part_3 = lax.optimization_barrier(
        (from_left, from_right, part_1, part_2, part_3)
    )
    w_parts = (part_0, part_1, part_2, part_3)

    def projected(*both):
        own, away = project(parts, both, w_qkv, w_parts)
        return own, moved(away, opposite_z)

    far_0 = moved(from_left[:half], right)
    far_1 = moved(from_right[half:], left)
    own_0, away_0 = projected(normed, swapped)
    own_1, away_1 = projected(from_left, moved(from_left, other_core))
    own_2, away_2 = projected(from_right, moved(from_right, other_core))
    far_0, far_1, away_0, own_1, own_2 = lax.optimization_barrier(
        (far_0, far_1, away_0, own_1, own_2)
    )
    both = (far_0, far_1, moved(far_0, other_core), moved(far_1, other_core))
    own_3, away_3 = project(parts, both, w_qkv, w_parts)

    places = []
    early = [own_0, own_1, own_2, own_3, away_0]
    for step, z_of in zip((0, 3, 1, 2, 0, 3, 1, 2), (z_high,) * 4 + (1 - z_high,) * 4):
        for core_of in (core, 1 - core):
            places.append((((x + step) % XS) * 2 + z_of) * 2 + core_of)
    place = jnp.stack(places).astype(jnp.int32)
    state = phase(place, [], early, [], False)
    away_3, state = lax.optimization_barrier((away_3, state))
    away_3 = moved(away_3, opposite_z)
    state = phase(place, early, [away_1, away_2], state, False)
    (head_outputs,) = phase(place, early + [away_1, away_2], [away_3], state, True)

    tokens = latent_tokens.shape[1]
    by_head = lax.all_to_all(
        head_outputs.reshape(-1, tokens, HEAD_DIM), "seq", split_axis=0, concat_axis=0, tiled=True
    )
    attended = by_head.transpose(1, 0, 2).reshape(1, tokens, -1)
    new_rows = update_rows(by_head, noisy_latents[0], w_out, 2 * YS)

    slot_index = z_low * YS + y
    source = lax.dynamic_index_in_dim(queue, slot_index, 0, keepdims=False)
    limit = lax.dynamic_index_in_dim(frame_counts, source, 0, keepdims=False)
    everyone = lax.all_to_all(
        new_rows, ("group", "dp"), split_axis=0, concat_axis=0, tiled=True
    )
    chosen = lax.dynamic_index_in_dim(everyone, source, 0, keepdims=False)
    line = chosen.shape[0] // 2
    seats = lax.axis_size("seq")
    up = [(i, i + 1) for i in range(seats - 1)]
    before = lax.ppermute(chosen[line:], "seq", up)
    after = lax.ppermute(chosen[:line], "seq", [(j, i) for i, j in up])
    decoded = causal_features(chosen, before, after, limit, conv_w, conv_b)
    return (attended, decoded[None])


def solution(mesh):
    return jax.shard_map(
        on_device,
        mesh=mesh,
        in_specs=(
            P(("group", "dp"), "seq", None),
            P(("group", "dp"), None, None),
            P(None, None, "seq"),
            P(),
            P(("group", "dp"), None, None, "seq", None),
            P(),
            P(),
            P(),
            P(),
        ),
        out_specs=(P(("group", "dp"), "seq", None), P(("group", "dp"), None, None, "seq", None)),
        check_vma=False,
    )
```

```python
import functools
import math

import jax
import jax.numpy as jnp
from jax import lax
from jax.experimental import pallas as pl
from jax.experimental.pallas import tpu as pltpu
from jax.sharding import PartitionSpec as P

HEAD_DIM = 128
EVERY = ("group", "seq", "dp")
XS, ZS, YS = (4, 4, 4)
VMEM_BYTES = 12 << 20
QUERY_SCALE = math.log2(math.e) / math.sqrt(HEAD_DIM)
TINY = pl.CostEstimate(flops=1, bytes_accessed=1, transcendentals=0)
NT = (((1,), (1,)), ((), ()))


def linear(x, y, z, core):
    return ((z % 2) * 16 + (x * 2 + z // 2) * 2 + core) * YS + y


def moved(array, move):
    perm = []
    for x in range(XS):
        for y in range(YS):
            for z in range(ZS):
                for core in range(2):
                    to = move(x, y, z, core)
                    there = linear(to[0] % XS, to[1] % YS, to[2] % ZS, to[3])
                    perm.append((linear(x, y, z, core), there))
    return lax.ppermute(array, EVERY, perm)


def right(x, y, z, core):
    return (x + 1, y, z, core)


def left(x, y, z, core):
    return (x - 1, y, z, core)


def other_core(x, y, z, core):
    return (x, y, z, 1 - core)


def opposite_z(x, y, z, core):
    return (x, y, z + 2, core)


def mirrored_z(x, y, z, core):
    return (x, y, 3 - z, core)


def project_kernel(n_tokens, part_ref, *refs):
    tokens = refs[:n_tokens]
    w_ref = refs[n_tokens]
    w_parts = refs[n_tokens + 1 : n_tokens + 5]
    own_ref, away_ref = refs[n_tokens + 5 :]

    def step(c, carry):
        total = None
        for k in range(4):
            depth = w_parts[k].shape[1]
            at = pl.multiple_of(part_ref[k] * depth, depth)
            rows = jnp.concatenate([t[:, pl.ds(at, depth)] for t in tokens], axis=0)
            columns = jnp.concatenate([w_ref[c, pl.ds(at, depth), :], w_parts[k][c]], axis=1)
            term = jnp.dot(rows, columns, preferred_element_type=jnp.float32)
            total = term if total is None else total + term
        total = (total * jnp.where(c == 0, QUERY_SCALE, 1.0)).astype(jnp.bfloat16)
        own_ref[c] = total[:, :HEAD_DIM]
        away_ref[c] = total[:, HEAD_DIM:]
        return carry

    lax.fori_loop(0, w_ref.shape[0], step, 0)


def project(parts, tokens, w_qkv, w_parts):
    rows = sum(t.shape[0] for t in tokens)
    depth = w_qkv.shape[1]
    vmem = pl.BlockSpec(memory_space=pltpu.VMEM)
    out = jax.ShapeDtypeStruct((3, rows, HEAD_DIM), jnp.bfloat16)
    return pl.pallas_call(
        functools.partial(project_kernel, len(tokens)),
        in_specs=[pl.BlockSpec(memory_space=pltpu.SMEM)] + [vmem] * (len(tokens) + 5),
        out_specs=[vmem, vmem],
        out_shape=(out, out),
        compiler_params=pltpu.CompilerParams(vmem_limit_bytes=VMEM_BYTES),
        cost_estimate=TINY,
    )(parts, *tokens, w_qkv, *w_parts)


def attend(q, blocks, state, chunk=256):
    ones = jnp.ones((chunk, HEAD_DIM), jnp.bfloat16)
    for block in blocks:
        for at in range(0, block.shape[1], chunk):
            keys = block[1, at : at + chunk, :]
            vals = jnp.concatenate([block[2, at : at + chunk, :], ones], axis=1)
            scores = lax.dot_general(q, keys, NT, preferred_element_type=jnp.float32)
            high = jnp.max(scores, axis=1, keepdims=True)
            if state is not None:
                high = jnp.maximum(state[0], high)
            probs = jnp.exp2(scores - high).astype(jnp.bfloat16)
            term = jnp.dot(probs, vals, preferred_element_type=jnp.float32)
            if state is not None:
                term = state[1] * jnp.exp2(state[0] - high) + term
            state = (high, term)
    return state


def finished(state):
    total = state[1]
    return (total[:, :HEAD_DIM] / total[:, HEAD_DIM:]).astype(jnp.bfloat16)


def phase_kernel(n_old, n_new, last, place_ref, *refs):
    old = refs[:n_old]
    new = refs[n_old : n_old + n_new]
    refs = refs[n_old + n_new :]
    q_all = refs[-1]
    rows = new[0].shape[1]
    for i, block in enumerate(old + new):
        q_all[i * rows : (i + 1) * rows, :] = block[0]
    owned = rows // 2
    run = owned // 2
    if n_old:
        top_ref, total_ref = refs[:2]
        refs = refs[2:]

    def put(at, state):
        size = state[1].shape[0]
        if last:
            outputs = finished(state)
            for i in range(size // run):
                piece = at // run + i
                to = place_ref[piece // 2] * owned + piece % 2 * run
                here = pl.ds(pl.multiple_of(to, run), run)
                refs[0][here, :] = outputs[i * run : (i + 1) * run]
        else:
            refs[0][pl.ds(at, size), :] = jnp.broadcast_to(state[0], (size, HEAD_DIM))
            refs[1][pl.ds(at, size), :] = state[1]

    def sweep(first, count, blocks, resumed):
        tiles = next(t for t in (1, 2, 4, 8) if count * rows // t <= 1280)
        size = count * rows // tiles

        def step(t, carry):
            at = pl.multiple_of(first * rows + t * size, run)
            here = pl.ds(at, size)
            state = None
            if resumed:
                state = (jnp.max(top_ref[here, :], axis=1, keepdims=True), total_ref[here, :])
            put(at, attend(q_all[here, :], blocks, state))
            return carry

        lax.fori_loop(0, tiles, step, 0)

    if n_old:
        sweep(0, n_old, new, True)
    sweep(n_old, n_new, old + new, False)


def phase(place, old, new, state, last):
    blocks = list(old) + list(new)
    tokens = sum(b.shape[1] for b in blocks)
    vmem = pl.BlockSpec(memory_space=pltpu.VMEM)
    if last:
        out_shape = [jax.ShapeDtypeStruct((tokens, HEAD_DIM), jnp.bfloat16)]
    else:
        out_shape = [
            jax.ShapeDtypeStruct((tokens, HEAD_DIM), jnp.float32),
            jax.ShapeDtypeStruct((tokens, 2 * HEAD_DIM), jnp.float32),
        ]
    return pl.pallas_call(
        functools.partial(phase_kernel, len(old), len(new), last),
        in_specs=[pl.BlockSpec(memory_space=pltpu.SMEM)] + [vmem] * (len(blocks) + len(state)),
        out_specs=[vmem] * len(out_shape),
        out_shape=out_shape,
        scratch_shapes=[pltpu.VMEM((tokens, HEAD_DIM), jnp.bfloat16)],
        compiler_params=pltpu.CompilerParams(vmem_limit_bytes=VMEM_BYTES),
        cost_estimate=TINY,
    )(place, *blocks, *state)


def update_kernel(att_ref, noisy_ref, w_ref, out_ref):
    heads, tokens, width = att_ref.shape
    squares = jnp.zeros((tokens, width), jnp.float32)
    for h in range(heads):
        values = att_ref[h].astype(jnp.float32)
        squares += values * values
    mean = jnp.sum(squares, axis=1, keepdims=True) / (heads * width)
    gain = lax.rsqrt(mean + 1e-06)
    predicted = jnp.zeros((w_ref.shape[0], tokens), jnp.float32)
    for h in range(heads):
        normed = (att_ref[h].astype(jnp.float32) * gain).astype(jnp.bfloat16)
        predicted += lax.dot_general(
            w_ref[:, h * width : (h + 1) * width], normed, NT, preferred_element_type=jnp.float32
        )
    half = predicted.shape[0] // 2
    both = jnp.concatenate([predicted[:half], predicted[half:]], axis=1)
    parts = []
    for _ in range(3):
        part = both.astype(jnp.bfloat16)
        both = both - part.astype(jnp.float32)
        parts.append(part)
    token = lax.broadcasted_iota(jnp.int32, (2 * tokens, 2 * tokens), 0)
    column = lax.broadcasted_iota(jnp.int32, (2 * tokens, 2 * tokens), 1)
    spread = jnp.where(token < tokens, 2 * token, 2 * token - 2 * tokens + 1) == column
    spread = jnp.where(spread, 1.0, 0.0).astype(jnp.bfloat16)
    grid = jnp.dot(jnp.concatenate(parts, axis=0), spread, preferred_element_type=jnp.float32)
    grid = grid[:half] + grid[half : 2 * half] + grid[2 * half :]
    channels = half // 2
    frames = 2 * tokens // 128
    for dy in range(2):
        for f in range(frames):
            at = (dy * frames + f) * channels
            rows = grid[dy * channels : (dy + 1) * channels, f * 128 : (f + 1) * 128]
            noisy = noisy_ref[at : at + channels, :].astype(jnp.float32)
            updated = (noisy + rows).astype(jnp.bfloat16)
            for i in range(out_ref.shape[0]):
                out_ref[i, at : at + channels, :] = updated


def update_rows(by_head, noisy, w_out, copies):
    channels, frames, rows, columns = noisy.shape
    noisy = noisy.transpose(2, 1, 0, 3).reshape(rows * frames * channels, columns)
    w_rows = w_out.T.reshape(channels, 2, 2, -1).transpose(2, 1, 0, 3).reshape(4 * channels, -1)
    return pl.pallas_call(
        update_kernel,
        in_specs=[pl.BlockSpec(memory_space=pltpu.VMEM)] * 3,
        out_specs=pl.BlockSpec(memory_space=pltpu.VMEM),
        out_shape=jax.ShapeDtypeStruct((copies,) + noisy.shape, jnp.bfloat16),
        compiler_params=pltpu.CompilerParams(vmem_limit_bytes=VMEM_BYTES),
        cost_estimate=TINY,
    )(by_head, noisy, w_rows)


def shifted_rows(rows):
    wide = rows.astype(jnp.float32)
    lane = lax.broadcasted_iota(jnp.int32, wide.shape, 1)
    from_left = jnp.where(lane == 0, 0.0, pltpu.roll(wide, 1, 1)).astype(jnp.bfloat16)
    from_right = jnp.where(lane == 127, 0.0, pltpu.roll(wide, 127, 1)).astype(jnp.bfloat16)
    return (from_left, rows, from_right)


def tap_product(w_ref, taps, lines, frames, channels):
    weights = []
    at = 0
    for dt in range(3):
        for dh, shifted in lines:
            first = (dt * 9 + dh * 3) * channels
            weights.append(w_ref[first : first + 3 * channels, :])
            for dw in range(3):
                for f in range(frames):
                    source = max(f + dt - 2, 0) * channels
                    taps[at : at + channels, f * 128 : (f + 1) * 128] = shifted[dw][
                        source : source + channels
                    ]
                at += channels
    return lax.dot_general(
        jnp.concatenate(weights, axis=0),
        taps[...],
        (((0,), (0,)), ((), ())),
        preferred_element_type=jnp.float32,
    )


def inner_kernel(rows_ref, w_ref, b_ref, out_ref, taps_0, taps_1):
    line = rows_ref.shape[0] // 2
    frames = out_ref.shape[2] // 128
    channels = line // frames
    upper = shifted_rows(rows_ref[:line, :])
    lower = shifted_rows(rows_ref[line:, :])
    for y, taps, lines in (
        (0, taps_0, ((1, upper), (2, lower))),
        (1, taps_1, ((0, upper), (1, lower))),
    ):
        out_ref[y] = tap_product(w_ref, taps, lines, frames, channels) + b_ref[...]


def halo_kernel(limit_ref, inner_ref, before_ref, after_ref, w_ref, out_ref, taps_0, taps_1):
    frames = inner_ref.shape[2] // 128
    channels = before_ref.shape[0] // frames
    features = []
    for y, taps, dh, ref in ((0, taps_0, 0, before_ref), (1, taps_1, 2, after_ref)):
        lines = ((dh, shifted_rows(ref[...])),)
        features.append(inner_ref[y] + tap_product(w_ref, taps, lines, frames, channels))
    blocks = []
    for f in range(frames):
        for y in range(2):
            block = features[y][:, f * 128 : (f + 1) * 128]
            blocks.append(jnp.where(f < limit_ref[0], block, 0.0))
    together = jnp.concatenate(blocks, axis=1)
    out_ref[...] = together.reshape(out_ref.shape).astype(jnp.bfloat16)


def inner_features(rows, conv_w, conv_b):
    outputs, depth = conv_w.shape
    vmem = pl.BlockSpec(memory_space=pltpu.VMEM)
    taps = pltpu.VMEM((depth * 2 // 3, 4 * rows.shape[1]), jnp.bfloat16)
    return pl.pallas_call(
        inner_kernel,
        in_specs=[vmem] * 3,
        out_specs=vmem,
        out_shape=jax.ShapeDtypeStruct((2, outputs, 4 * rows.shape[1]), jnp.float32),
        scratch_shapes=[taps, taps],
        compiler_params=pltpu.CompilerParams(vmem_limit_bytes=VMEM_BYTES),
        cost_estimate=TINY,
    )(rows, conv_w.T, conv_b[:, None])


def all_features(inner, before, after, limit, conv_w):
    outputs, depth = conv_w.shape
    columns = before.shape[1]
    vmem = pl.BlockSpec(memory_space=pltpu.VMEM)
    taps = pltpu.VMEM((depth // 3, 4 * columns), jnp.bfloat16)
    out = pl.pallas_call(
        halo_kernel,
        in_specs=[pl.BlockSpec(memory_space=pltpu.SMEM)] + [vmem] * 4,
        out_specs=vmem,
        out_shape=jax.ShapeDtypeStruct((outputs, 8, columns), jnp.bfloat16),
        scratch_shapes=[taps, taps],
        compiler_params=pltpu.CompilerParams(vmem_limit_bytes=VMEM_BYTES),
        cost_estimate=TINY,
    )(limit[None], inner, before, after, conv_w.T)
    return out.reshape(outputs, 4, 2, columns)


def on_device(
    latent_tokens, modulation, w_qkv, w_out, noisy_latents, queue, frame_counts, conv_w, conv_b
):
    z_low = lax.axis_index("group")
    seat = lax.axis_index("seq")
    y = lax.axis_index("dp")
    x, z_high, core = (seat // 4, seat // 2 % 2, seat % 2)

    quarter = w_qkv.shape[1] // 4
    part_0 = moved(lax.dynamic_slice_in_dim(w_qkv, y * quarter, quarter, axis=1), mirrored_z)
    part_2 = lax.dynamic_slice_in_dim(w_qkv, (y + 2) % 4 * quarter, quarter, axis=1)
    parts = (y + jnp.arange(4, dtype=jnp.int32)) % 4

    values = latent_tokens[0].astype(jnp.float32)
    shift_scale = modulation[0]
    scaled = values * lax.rsqrt(jnp.mean(values * values, axis=-1, keepdims=True) + 1e-06)
    normed = (scaled * (1.0 + shift_scale[1]) + shift_scale[0]).astype(jnp.bfloat16)

    half = normed.shape[0] // 2
    from_left = moved(normed, right)
    from_right = moved(normed, left)
    swapped = moved(normed, other_core)
    part_0, part_2, swapped = lax.optimization_barrier((part_0, part_2, swapped))
    part_2 = moved(part_2, mirrored_z)
    part_1 = moved(part_0, lambda x, y, z, core: (x, y - 1, z, core))
    part_3 = moved(part_0, lambda x, y, z, core: (x, y + 1, z, core))
    near_0 = from_left[:half]
    near_1 = from_right[half:]
    near_0, near_1, from_left, from_right, part_1, part_2, part_3 = lax.optimization_barrier(
        (near_0, near_1, from_left, from_right, part_1, part_2, part_3)
    )
    w_parts = (part_0, part_1, part_2, part_3)

    def projected(*both):
        own, away = project(parts, both, w_qkv, w_parts)
        return own, moved(away, opposite_z)

    far_0 = moved(near_0, right)
    far_1 = moved(near_1, left)
    own_0, away_0 = projected(normed, swapped)
    own_1, away_1 = projected(from_left, moved(from_left, other_core))
    own_2, away_2 = projected(from_right, moved(from_right, other_core))
    far_0, far_1, away_0, own_1, own_2 = lax.optimization_barrier(
        (far_0, far_1, away_0, own_1, own_2)
    )
    both = (far_0, far_1, moved(far_0, other_core), moved(far_1, other_core))
    own_3, away_3 = project(parts, both, w_qkv, w_parts)

    places = []
    early = [own_0, own_1, own_2, own_3, away_0]
    for step, z_of in zip((0, 3, 1, 2, 0, 3, 1, 2), (z_high,) * 4 + (1 - z_high,) * 4):
        for core_of in (core, 1 - core):
            places.append((((x + step) % XS) * 2 + z_of) * 2 + core_of)
    place = jnp.stack(places).astype(jnp.int32)
    state = phase(place, [], early, [], False)
    away_3, state = lax.optimization_barrier((away_3, state))
    away_3 = moved(away_3, opposite_z)
    state = phase(place, early, [away_1, away_2], state, False)
    (head_outputs,) = phase(place, early + [away_1, away_2], [away_3], state, True)

    tokens = latent_tokens.shape[1]
    by_head = lax.all_to_all(
        head_outputs.reshape(-1, tokens, HEAD_DIM), "seq", split_axis=0, concat_axis=0, tiled=True
    )
    attended = by_head.transpose(1, 0, 2).reshape(1, tokens, -1)
    new_rows = update_rows(by_head, noisy_latents[0], w_out, 2 * YS)

    slot_index = z_low * YS + y
    source = lax.dynamic_index_in_dim(queue, slot_index, 0, keepdims=False)
    limit = lax.dynamic_index_in_dim(frame_counts, source, 0, keepdims=False)
    everyone = lax.all_to_all(
        new_rows, ("group", "dp"), split_axis=0, concat_axis=0, tiled=True
    )
    chosen = lax.dynamic_index_in_dim(everyone, source, 0, keepdims=False)
    line = chosen.shape[0] // 2
    seats = lax.axis_size("seq")
    up = [(i, i + 1) for i in range(seats - 1)]
    before = lax.ppermute(chosen[line:], "seq", up)
    after = lax.ppermute(chosen[:line], "seq", [(j, i) for i, j in up])
    inner = inner_features(chosen, conv_w, conv_b)
    decoded = all_features(inner, before, after, limit, conv_w)
    return (attended, decoded[None])


def solution(mesh):
    return jax.shard_map(
        on_device,
        mesh=mesh,
        in_specs=(
            P(("group", "dp"), "seq", None),
            P(("group", "dp"), None, None),
            P(None, None, "seq"),
            P(),
            P(("group", "dp"), None, None, "seq", None),
            P(),
            P(),
            P(),
            P(),
        ),
        out_specs=(P(("group", "dp"), "seq", None), P(("group", "dp"), None, None, "seq", None)),
        check_vma=False,
    )
```

```python
import functools
import math

import jax
import jax.numpy as jnp
from jax import lax
from jax.experimental import pallas as pl
from jax.experimental.pallas import tpu as pltpu
from jax.sharding import PartitionSpec as P

HEAD_DIM = 128
EVERY = ("group", "seq", "dp")
XS, ZS, YS = (4, 4, 4)
VMEM_BYTES = 12 << 20
QUERY_SCALE = math.log2(math.e) / math.sqrt(HEAD_DIM)
TINY = pl.CostEstimate(flops=1, bytes_accessed=1, transcendentals=0)
NT = (((1,), (1,)), ((), ()))


def linear(x, y, z, core):
    return ((z % 2) * 16 + (x * 2 + z // 2) * 2 + core) * YS + y


def moved(array, move):
    perm = []
    for x in range(XS):
        for y in range(YS):
            for z in range(ZS):
                for core in range(2):
                    to = move(x, y, z, core)
                    there = linear(to[0] % XS, to[1] % YS, to[2] % ZS, to[3])
                    perm.append((linear(x, y, z, core), there))
    return lax.ppermute(array, EVERY, perm)


def right(x, y, z, core):
    return (x + 1, y, z, core)


def left(x, y, z, core):
    return (x - 1, y, z, core)


def other_core(x, y, z, core):
    return (x, y, z, 1 - core)


def opposite_z(x, y, z, core):
    return (x, y, z + 2, core)


def mirrored_z(x, y, z, core):
    return (x, y, 3 - z, core)


def project_kernel(n_tokens, part_ref, *refs):
    tokens = refs[:n_tokens]
    w_ref = refs[n_tokens]
    w_parts = refs[n_tokens + 1 : n_tokens + 5]
    own_ref, away_ref = refs[n_tokens + 5 :]
    for c in range(w_ref.shape[0]):
        total = None
        for k in range(4):
            depth = w_parts[k].shape[1]
            at = pl.multiple_of(part_ref[k] * depth, depth)
            rows = jnp.concatenate([t[:, pl.ds(at, depth)] for t in tokens], axis=0)
            columns = jnp.concatenate([w_ref[c, pl.ds(at, depth), :], w_parts[k][c]], axis=1)
            term = jnp.dot(rows, columns, preferred_element_type=jnp.float32)
            total = term if total is None else total + term
        if c == 0:
            total = total * QUERY_SCALE
        total = total.astype(jnp.bfloat16)
        own_ref[c] = total[:, :HEAD_DIM]
        away_ref[c] = total[:, HEAD_DIM:]


def project(parts, tokens, w_qkv, w_parts):
    rows = sum(t.shape[0] for t in tokens)
    depth = w_qkv.shape[1]
    vmem = pl.BlockSpec(memory_space=pltpu.VMEM)
    out = jax.ShapeDtypeStruct((3, rows, HEAD_DIM), jnp.bfloat16)
    return pl.pallas_call(
        functools.partial(project_kernel, len(tokens)),
        in_specs=[pl.BlockSpec(memory_space=pltpu.SMEM)] + [vmem] * (len(tokens) + 5),
        out_specs=[vmem, vmem],
        out_shape=(out, out),
        compiler_params=pltpu.CompilerParams(vmem_limit_bytes=VMEM_BYTES),
        cost_estimate=TINY,
    )(parts, *tokens, w_qkv, *w_parts)


def attend(q, blocks, state, chunk=256):
    ones = jnp.ones((chunk, HEAD_DIM), jnp.bfloat16)
    for block in blocks:
        for at in range(0, block.shape[1], chunk):
            keys = block[1, at : at + chunk, :]
            vals = jnp.concatenate([block[2, at : at + chunk, :], ones], axis=1)
            scores = lax.dot_general(q, keys, NT, preferred_element_type=jnp.float32)
            high = jnp.max(scores, axis=1, keepdims=True)
            if state is not None:
                high = jnp.maximum(state[0], high)
            probs = jnp.exp2(scores - high).astype(jnp.bfloat16)
            term = jnp.dot(probs, vals, preferred_element_type=jnp.float32)
            if state is not None:
                term = state[1] * jnp.exp2(state[0] - high) + term
            state = (high, term)
    return state


def finished(state):
    total = state[1]
    return (total[:, :HEAD_DIM] / total[:, HEAD_DIM:]).astype(jnp.bfloat16)


def phase_kernel(n_old, n_new, last, place_ref, *refs):
    old = refs[:n_old]
    new = refs[n_old : n_old + n_new]
    refs = refs[n_old + n_new :]
    q_all = refs[-1]
    rows = new[0].shape[1]
    for i, block in enumerate(old + new):
        q_all[i * rows : (i + 1) * rows, :] = block[0]
    owned = rows // 2
    run = owned // 2
    if n_old:
        top_ref, total_ref = refs[:2]
        refs = refs[2:]

    def put(at, state):
        size = state[1].shape[0]
        if last:
            outputs = finished(state)
            for i in range(size // run):
                piece = at // run + i
                to = place_ref[piece // 2] * owned + piece % 2 * run
                here = pl.ds(pl.multiple_of(to, run), run)
                refs[0][here, :] = outputs[i * run : (i + 1) * run]
        else:
            refs[0][pl.ds(at, size), :] = jnp.broadcast_to(state[0], (size, HEAD_DIM))
            refs[1][pl.ds(at, size), :] = state[1]

    def sweep(first, count, blocks, resumed):
        tiles = next(t for t in (1, 2, 4, 8) if count * rows // t <= 1280)
        size = count * rows // tiles

        def step(t, carry):
            at = pl.multiple_of(first * rows + t * size, run)
            here = pl.ds(at, size)
            state = None
            if resumed:
                state = (jnp.max(top_ref[here, :], axis=1, keepdims=True), total_ref[here, :])
            put(at, attend(q_all[here, :], blocks, state))
            return carry

        lax.fori_loop(0, tiles, step, 0)

    if n_old:
        sweep(0, n_old, new, True)
    sweep(n_old, n_new, old + new, False)


def phase(place, old, new, state, last):
    blocks = list(old) + list(new)
    tokens = sum(b.shape[1] for b in blocks)
    vmem = pl.BlockSpec(memory_space=pltpu.VMEM)
    if last:
        out_shape = [jax.ShapeDtypeStruct((tokens, HEAD_DIM), jnp.bfloat16)]
    else:
        out_shape = [
            jax.ShapeDtypeStruct((tokens, HEAD_DIM), jnp.float32),
            jax.ShapeDtypeStruct((tokens, 2 * HEAD_DIM), jnp.float32),
        ]
    return pl.pallas_call(
        functools.partial(phase_kernel, len(old), len(new), last),
        in_specs=[pl.BlockSpec(memory_space=pltpu.SMEM)] + [vmem] * (len(blocks) + len(state)),
        out_specs=[vmem] * len(out_shape),
        out_shape=out_shape,
        scratch_shapes=[pltpu.VMEM((tokens, HEAD_DIM), jnp.bfloat16)],
        compiler_params=pltpu.CompilerParams(vmem_limit_bytes=VMEM_BYTES),
        cost_estimate=TINY,
    )(place, *blocks, *state)


def update_kernel(att_ref, noisy_ref, w_ref, out_ref):
    heads, tokens, width = att_ref.shape
    squares = jnp.zeros((tokens, width), jnp.float32)
    for h in range(heads):
        values = att_ref[h].astype(jnp.float32)
        squares += values * values
    mean = jnp.sum(squares, axis=1, keepdims=True) / (heads * width)
    gain = lax.rsqrt(mean + 1e-06)
    predicted = jnp.zeros((w_ref.shape[0], tokens), jnp.float32)
    for h in range(heads):
        normed = (att_ref[h].astype(jnp.float32) * gain).astype(jnp.bfloat16)
        predicted += lax.dot_general(
            w_ref[:, h * width : (h + 1) * width], normed, NT, preferred_element_type=jnp.float32
        )
    half = predicted.shape[0] // 2
    both = jnp.concatenate([predicted[:half], predicted[half:]], axis=1)
    parts = []
    for _ in range(3):
        part = both.astype(jnp.bfloat16)
        both = both - part.astype(jnp.float32)
        parts.append(part)
    token = lax.broadcasted_iota(jnp.int32, (2 * tokens, 2 * tokens), 0)
    column = lax.broadcasted_iota(jnp.int32, (2 * tokens, 2 * tokens), 1)
    spread = jnp.where(token < tokens, 2 * token, 2 * token - 2 * tokens + 1) == column
    spread = jnp.where(spread, 1.0, 0.0).astype(jnp.bfloat16)
    grid = jnp.dot(jnp.concatenate(parts, axis=0), spread, preferred_element_type=jnp.float32)
    grid = grid[:half] + grid[half : 2 * half] + grid[2 * half :]
    channels = half // 2
    frames = 2 * tokens // 128
    for dy in range(2):
        for f in range(frames):
            at = (dy * frames + f) * channels
            rows = grid[dy * channels : (dy + 1) * channels, f * 128 : (f + 1) * 128]
            noisy = noisy_ref[at : at + channels, :].astype(jnp.float32)
            updated = (noisy + rows).astype(jnp.bfloat16)
            for i in range(out_ref.shape[0]):
                out_ref[i, at : at + channels, :] = updated


def update_rows(by_head, noisy, w_out, copies):
    channels, frames, rows, columns = noisy.shape
    noisy = noisy.transpose(2, 1, 0, 3).reshape(rows * frames * channels, columns)
    w_rows = w_out.T.reshape(channels, 2, 2, -1).transpose(2, 1, 0, 3).reshape(4 * channels, -1)
    return pl.pallas_call(
        update_kernel,
        in_specs=[pl.BlockSpec(memory_space=pltpu.VMEM)] * 3,
        out_specs=pl.BlockSpec(memory_space=pltpu.VMEM),
        out_shape=jax.ShapeDtypeStruct((copies,) + noisy.shape, jnp.bfloat16),
        compiler_params=pltpu.CompilerParams(vmem_limit_bytes=VMEM_BYTES),
        cost_estimate=TINY,
    )(by_head, noisy, w_rows)


def features_kernel(limit_ref, rows_ref, before_ref, after_ref, w_ref, b_ref, out_ref, taps):
    frames, channels = (4, 16)
    line = frames * channels
    four = jnp.concatenate([before_ref[...], rows_ref[...], after_ref[...]], axis=0)
    wide = four.astype(jnp.float32)
    lane = lax.broadcasted_iota(jnp.int32, wide.shape, 1)
    from_left = jnp.where(lane == 0, 0.0, pltpu.roll(wide, 1, 1)).astype(jnp.bfloat16)
    from_right = jnp.where(lane == 127, 0.0, pltpu.roll(wide, 127, 1)).astype(jnp.bfloat16)
    shifted = (from_left, four, from_right)
    for dt in range(3):
        for dh in range(3):
            for dw in range(3):
                tap = (dt * 3 + dh) * 3 + dw
                for f in range(frames):
                    for y in range(2):
                        at = (y + dh) * line + max(f + dt - 2, 0) * channels
                        block = (f * 2 + y) * 128
                        taps[tap * channels : (tap + 1) * channels, block : block + 128] = shifted[
                            dw
                        ][at : at + channels]
    features = lax.dot_general(
        w_ref[...], taps[...], (((0,), (0,)), ((), ())), preferred_element_type=jnp.float32
    )
    features = features + b_ref[...]
    frame = lax.broadcasted_iota(jnp.int32, features.shape, 1) // 256
    features = jnp.where(frame < limit_ref[0], features, 0.0)
    out_ref[...] = features.reshape(out_ref.shape).astype(jnp.bfloat16)


def causal_features(rows, before, after, limit, conv_w, conv_b):
    outputs, depth = conv_w.shape
    columns = rows.shape[1]
    vmem = pl.BlockSpec(memory_space=pltpu.VMEM)
    out = pl.pallas_call(
        features_kernel,
        in_specs=[pl.BlockSpec(memory_space=pltpu.SMEM)] + [vmem] * 5,
        out_specs=vmem,
        out_shape=jax.ShapeDtypeStruct((outputs, 8, columns), jnp.bfloat16),
        scratch_shapes=[pltpu.VMEM((depth, 8 * columns), jnp.bfloat16)],
        compiler_params=pltpu.CompilerParams(vmem_limit_bytes=VMEM_BYTES),
        cost_estimate=TINY,
    )(limit[None], rows, before, after, conv_w.T, conv_b[:, None])
    return out.reshape(outputs, 4, 2, columns)


def on_device(
    latent_tokens, modulation, w_qkv, w_out, noisy_latents, queue, frame_counts, conv_w, conv_b
):
    z_low = lax.axis_index("group")
    seat = lax.axis_index("seq")
    y = lax.axis_index("dp")
    x, z_high, core = (seat // 4, seat // 2 % 2, seat % 2)

    quarter = w_qkv.shape[1] // 4
    part_0 = moved(lax.dynamic_slice_in_dim(w_qkv, y * quarter, quarter, axis=1), mirrored_z)
    part_2 = lax.dynamic_slice_in_dim(w_qkv, (y + 2) % 4 * quarter, quarter, axis=1)
    parts = (y + jnp.arange(4, dtype=jnp.int32)) % 4

    values = latent_tokens[0].astype(jnp.float32)
    shift_scale = modulation[0]
    scaled = values * lax.rsqrt(jnp.mean(values * values, axis=-1, keepdims=True) + 1e-06)
    normed = (scaled * (1.0 + shift_scale[1]) + shift_scale[0]).astype(jnp.bfloat16)

    half = normed.shape[0] // 2
    from_left = moved(normed, right)
    from_right = moved(normed, left)
    swapped = moved(normed, other_core)
    part_0, part_2, swapped = lax.optimization_barrier((part_0, part_2, swapped))
    part_2 = moved(part_2, mirrored_z)
    part_1 = moved(part_0, lambda x, y, z, core: (x, y - 1, z, core))
    part_3 = moved(part_0, lambda x, y, z, core: (x, y + 1, z, core))
    near_0 = from_left[:half]
    near_1 = from_right[half:]
    near_0, near_1, from_left, from_right, part_1, part_2, part_3 = lax.optimization_barrier(
        (near_0, near_1, from_left, from_right, part_1, part_2, part_3)
    )
    w_parts = (part_0, part_1, part_2, part_3)

    def projected(*both):
        own, away = project(parts, both, w_qkv, w_parts)
        return own, moved(away, opposite_z)

    far_0 = moved(near_0, right)
    far_1 = moved(near_1, left)
    own_0, away_0 = projected(normed, swapped)
    own_1, away_1 = projected(from_left, moved(from_left, other_core))
    own_2, away_2 = projected(from_right, moved(from_right, other_core))
    far_0, far_1, away_0, own_1, own_2 = lax.optimization_barrier(
        (far_0, far_1, away_0, own_1, own_2)
    )
    both = (far_0, far_1, moved(far_0, other_core), moved(far_1, other_core))
    own_3, away_3 = project(parts, both, w_qkv, w_parts)

    places = []
    early = [own_0, own_1, own_2, own_3, away_0]
    for step, z_of in zip((0, 3, 1, 2, 0, 3, 1, 2), (z_high,) * 4 + (1 - z_high,) * 4):
        for core_of in (core, 1 - core):
            places.append((((x + step) % XS) * 2 + z_of) * 2 + core_of)
    place = jnp.stack(places).astype(jnp.int32)
    state = phase(place, [], early, [], False)
    away_3, state = lax.optimization_barrier((away_3, state))
    away_3 = moved(away_3, opposite_z)
    state = phase(place, early, [away_1, away_2], state, False)
    (head_outputs,) = phase(place, early + [away_1, away_2], [away_3], state, True)

    tokens = latent_tokens.shape[1]
    by_head = lax.all_to_all(
        head_outputs.reshape(-1, tokens, HEAD_DIM), "seq", split_axis=0, concat_axis=0, tiled=True
    )
    attended = by_head.transpose(1, 0, 2).reshape(1, tokens, -1)
    new_rows = update_rows(by_head, noisy_latents[0], w_out, 2 * YS)

    slot_index = z_low * YS + y
    source = lax.dynamic_index_in_dim(queue, slot_index, 0, keepdims=False)
    limit = lax.dynamic_index_in_dim(frame_counts, source, 0, keepdims=False)
    everyone = lax.all_to_all(
        new_rows, ("group", "dp"), split_axis=0, concat_axis=0, tiled=True
    )
    chosen = lax.dynamic_index_in_dim(everyone, source, 0, keepdims=False)
    line = chosen.shape[0] // 2
    seats = lax.axis_size("seq")
    up = [(i, i + 1) for i in range(seats - 1)]
    before = lax.ppermute(chosen[line:], "seq", up)
    after = lax.ppermute(chosen[:line], "seq", [(j, i) for i, j in up])
    decoded = causal_features(chosen, before, after, limit, conv_w, conv_b)
    return (attended, decoded[None])


def solution(mesh):
    return jax.shard_map(
        on_device,
        mesh=mesh,
        in_specs=(
            P(("group", "dp"), "seq", None),
            P(("group", "dp"), None, None),
            P(None, None, "seq"),
            P(),
            P(("group", "dp"), None, None, "seq", None),
            P(),
            P(),
            P(),
            P(),
        ),
        out_specs=(P(("group", "dp"), "seq", None), P(("group", "dp"), None, None, "seq", None)),
        check_vma=False,
    )
```
